32 devices in a mesh: ctx: 4 (over y, core), tp: 4 (over z), pp: 2 (over x).
Axes of the slice: x: 2, y: 2, z: 4, core: 2. Of those that a mesh axis runs over, the one named last changes fastest.
Arguments:
- queries: bfloat16 [2, 1024, 12288], P('pp', 'ctx', 'tp'), may hold values from -8 to 8
- latents: bfloat16 [2, 1024, 576], P('pp', ('ctx', 'tp')), may hold values from -8 to 8
- latent_gain: float32 [2, 512], P('pp'), may hold values from 0.5 to 2
- w_ukv: bfloat16 [2, 512, 16384], P('pp', None, 'tp'), may hold values from -0.25 to 0.25
- w_o: bfloat16 [2, 8192, 7168], P('pp', 'tp'), may hold values from -0.1875 to 0.1875
- residual: bfloat16 [2, 1024, 7168], P('pp', ('ctx', 'tp')), may hold values from -3 to 3
- block_order: int32 [2, 8], P('pp'), may hold values from 0 to 7, each once within a row
Outputs:
- handed: bfloat16 [2, 1024, 7168], P('pp', ('ctx', 'tp'))
The draws below stay inside these ranges and needn't reach their ends.
Inputs may be any that keep to these rules, and one draw needn't show every extreme that they name: `block_order`: each row names each of the 8 sequence blocks once.
All inputs are finite; a program needn't handle non-finite values.
Results may differ from the reference program's by a relative error of at most 0.02.
Values may be sent and summed in bfloat16 or wider, within the bound.
No kernel may reach another device: no remote copies, remote signals or barrier semaphores. Data moves between devices by JAX's collectives and lax.ppermute only.
A program may use at most 128 MiB of HBM per device.

```python
import math
import jax
import jax.numpy as jnp
from jax import lax

D = 7168
HEADS = 64
NOPE = 128
ROPE = 64
VDIM = 128
LATENT = 512
TOKENS = 1024
BLOCKS = 8
BLOCK_LEN = 128
SEGMENTS = 2


def latent_table(key):
    base = jax.random.fold_in(key, 101)
    keys = jax.random.split(base, 4)
    row_scale = jnp.exp(jax.random.uniform(keys[0], (SEGMENTS, TOKENS, 1), minval=math.log(0.3), maxval=math.log(3.0)))
    col_scale = jnp.exp(jax.random.uniform(keys[1], (SEGMENTS, 1, LATENT), minval=math.log(0.3), maxval=math.log(3.0)))
    compressed = jax.random.normal(keys[2], (SEGMENTS, TOKENS, LATENT)) * row_scale * col_scale
    compressed = jnp.clip(compressed, -8.0, 8.0)
    rope_raw = jnp.clip(jax.random.normal(keys[3], (SEGMENTS, TOKENS, ROPE)), -8.0, 8.0)
    return (compressed, rope_raw)


def draw_latents(key, part):
    compressed, rope_raw = latent_table(key)
    return jnp.concatenate([compressed, rope_raw], axis=-1).astype(jnp.bfloat16)


def draw_queries(key, part):
    base = jax.random.fold_in(key, 202)
    drawn = jnp.clip(jax.random.normal(base, (SEGMENTS, TOKENS, HEADS, NOPE + ROPE)), -8.0, 8.0)
    return drawn.reshape(SEGMENTS, TOKENS, HEADS * (NOPE + ROPE)).astype(jnp.bfloat16)


def levels(rng, dims, shards, smallest, high):
    level = 1.0
    for dim, parts in shards:
        heights = jax.random.uniform(jax.random.fold_in(jax.random.fold_in(rng, 6), dim), (parts,), jnp.float32, smallest / len(shards), high / len(shards))
        level = level * jnp.repeat(jnp.exp(heights), dims[dim] // parts).reshape((-1,) + (1,) * (len(dims) - 1 - dim))
    return level


def noise(rng, dims, spread, reach, pieces=(), kind=jnp.bfloat16):
    values = jax.random.normal(rng, dims, jnp.float32) * spread
    if len(pieces) > 0:
        values = levels(rng, dims, pieces, -0.22, 0.18) * values
    return jnp.clip(values, min=-reach, max=reach).astype(kind)


def setup_inputs(seed: int = 0) -> dict:
    key_list = jax.random.split(jax.random.key(seed), 8)
    queries = draw_queries(jax.random.fold_in(key_list[7], 71), 0)
    latents = draw_latents(jax.random.fold_in(key_list[7], 71), 0)
    latent_gain = jnp.clip(jnp.exp(math.log(2.0) - 1.3862944 * jax.random.uniform(key_list[2], (SEGMENTS, LATENT), jnp.float32) ** levels(key_list[2], (SEGMENTS, LATENT), ((0, 2),), -0.2, 0.2)), 0.5, 2.0)
    w_ukv = noise(key_list[3], (SEGMENTS, LATENT, HEADS * (NOPE + VDIM)), LATENT ** -0.5, 0.25, ((0, 2), (2, 4)))
    w_o = noise(key_list[4], (SEGMENTS, HEADS * VDIM, D), (HEADS * VDIM // 8) ** -0.5, 0.1875, ((0, 2), (1, 4)))
    residual = noise(key_list[5], (SEGMENTS, TOKENS, D), 0.5, 3.0, ((0, 2), (1, 16)))
    block_order = jax.vmap(lambda own: jax.random.permutation(own, BLOCKS))(jax.random.split(key_list[6], SEGMENTS)).reshape((SEGMENTS, BLOCKS)).astype(jnp.int32)
    return dict(queries=queries, latents=latents, latent_gain=latent_gain, w_ukv=w_ukv, w_o=w_o, residual=residual, block_order=block_order)


score_scale = 0.135

def rotate(values, places):
    middle = values.shape[-1] // 2
    freqs = 10000.0 ** (-(jnp.arange(middle).astype(jnp.float32) * 2.0 / values.shape[-1]))
    angles = places[..., None] * freqs
    first_half = values[..., :middle]
    second_half = values[..., middle:]
    return jnp.concatenate([first_half * jnp.cos(angles) - second_half * jnp.sin(angles), first_half * jnp.sin(angles) + second_half * jnp.cos(angles)], axis=-1)

def reference(queries, latents, latent_gain, w_ukv, w_o, residual, block_order):
    outputs = []
    for segment in range(SEGMENTS):
        row_ids = jnp.arange(TOKENS, dtype=jnp.int32)
        places = block_order[segment][row_ids // BLOCK_LEN] * BLOCK_LEN + row_ids % BLOCK_LEN
        angles_at = places.astype(jnp.float32)
        latent_rows = latents[segment].astype(jnp.float32)
        compressed = latent_rows[:, :LATENT]
        scale_rows = lax.rsqrt(lax.optimization_barrier(jnp.mean(compressed * compressed, axis=-1, keepdims=True)) + 1e-06)
        normed = (compressed * scale_rows * latent_gain[segment][None, :]).astype(jnp.bfloat16)
        key_rope = rotate(latent_rows[:, LATENT:], angles_at).astype(jnp.bfloat16)
        query_all = queries[segment].reshape(TOKENS, HEADS, NOPE + ROPE)
        query_nope = jnp.moveaxis(query_all[..., :NOPE], 1, 0)
        query_rope = jnp.moveaxis(rotate(query_all[..., NOPE:].astype(jnp.float32), angles_at[:, None]).astype(jnp.bfloat16), 1, 0)
        head_weights = jnp.moveaxis(w_ukv[segment].reshape(LATENT, HEADS, NOPE + VDIM), 1, 0)
        allowed = places[None, :] <= places[:, None]

        def one_head(inputs):
            weight_head, nope_part, rope_part = inputs
            key_value = jnp.dot(normed, weight_head, preferred_element_type=jnp.float32).astype(jnp.bfloat16)
            scores = (jnp.dot(nope_part, key_value[:, :NOPE].T, preferred_element_type=jnp.float32) + jnp.dot(rope_part, key_rope.T, preferred_element_type=jnp.float32)) * score_scale
            scores = jnp.where(allowed, scores, -1e+30)
            row_top = lax.optimization_barrier(jnp.max(scores, axis=-1, keepdims=True))
            weights = jnp.where(allowed, jnp.exp(scores - row_top), 0.0)
            totals = lax.optimization_barrier(jnp.sum(weights, axis=-1, keepdims=True))
            summed = jnp.dot(weights.astype(jnp.bfloat16), key_value[:, NOPE:], preferred_element_type=jnp.float32)
            return (summed / totals).astype(jnp.bfloat16)
        heads_out = lax.map(one_head, (head_weights, query_nope, query_rope))
        attention = jnp.moveaxis(heads_out, 0, 1).reshape(TOKENS, HEADS * VDIM)
        projected = jnp.dot(attention, w_o[segment], preferred_element_type=jnp.float32)
        outputs.append((projected + residual[segment].astype(jnp.float32)).astype(jnp.bfloat16))
    return jnp.roll(jnp.stack(outputs), 1, axis=0)
```

```python
import functools
import math

import jax
import jax.numpy as jnp
from jax import lax
from jax.experimental import pallas as pl
from jax.experimental.pallas import tpu as pltpu
from jax.sharding import PartitionSpec as P

NOPE = 128
ROPE = 64
VDIM = 128
LATENT = 512
LANES = 128

score_scale = 0.135
SCALE2 = score_scale * math.log2(math.e)

UNIT_PIECES = {0: 2, 1: 2}


def angles_of(places):
    freqs = 10000.0 ** (-(jnp.arange(ROPE // 2).astype(jnp.float32) * 2.0 / ROPE))
    return places.astype(jnp.float32)[:, None] * freqs


def rotate(values, places):
    middle = values.shape[-1] // 2
    angles = angles_of(places)
    first_half = values[..., :middle]
    second_half = values[..., middle:]
    return jnp.concatenate(
        [
            first_half * jnp.cos(angles) - second_half * jnp.sin(angles),
            first_half * jnp.sin(angles) + second_half * jnp.cos(angles),
        ],
        axis=-1,
    )


def place_rows(order_row, first, count, block_len):
    row_ids = first + jnp.arange(count, dtype=jnp.int32)
    owners = row_ids // block_len
    table = jnp.arange(order_row.shape[0], dtype=jnp.int32)
    base = jnp.sum(jnp.where(owners[:, None] == table[None, :], order_row[None, :], 0), axis=1)
    return base * block_len + row_ids % block_len


def gather_keys(own_keys):
    tp_count, ctx_count = lax.axis_size("tp"), lax.axis_size("ctx")
    steps = []
    step = 1
    while step < tp_count:
        steps.append(("tp", step))
        step *= 2
    step = 2
    while step < ctx_count:
        steps.append(("ctx", step))
        step *= 2
    steps.append(("ctx", 1))
    held, masks = own_keys, [(0, 0)]
    for axis, step in steps:
        pairs = [(i, i ^ step) for i in range(lax.axis_size(axis))]
        got = lax.ppermute(held, axis, pairs)
        held = jnp.concatenate([held, got], axis=0)
        masks = masks + [
            (c ^ step, t) if axis == "ctx" else (c, t ^ step) for c, t in masks
        ]
    return held, masks


def attention_kernel(q_ref, lat_ref, w_ref, cos_ref, sin_up_ref, sin_down_ref, qpos_ref, kpos_ref, out_ref, bias_ref):
    @pl.when(pl.program_id(0) == 0)
    def _():
        bias_ref[...] = jnp.where(kpos_ref[...] <= qpos_ref[...], 0.0, -1e30)

    normed = lat_ref[:, :LATENT]
    key_rope = lat_ref[:, LATENT:]
    rows = q_ref.shape[0]
    produced = jnp.dot(normed, w_ref[...], preferred_element_type=jnp.float32).astype(jnp.bfloat16)
    ones = jnp.ones((lat_ref.shape[0], LANES), jnp.bfloat16)
    keys, values = [], []
    for h in range(2):
        base = h * (NOPE + VDIM)
        keys.append(jnp.concatenate([produced[:, base : base + NOPE], key_rope], axis=1))
        values.append(jnp.concatenate([produced[:, base + NOPE : base + NOPE + VDIM], ones], axis=1))
    chunk = min(rows, 128)
    for r in range(rows // chunk):
        span = pl.ds(r * chunk, chunk)
        g0 = q_ref[span, :LANES]
        g1 = q_ref[span, LANES : 2 * LANES].astype(jnp.float32)
        g2 = q_ref[span, 2 * LANES :].astype(jnp.float32)
        r1 = pltpu.roll(g1, ROPE, 1)
        r2 = pltpu.roll(g2, ROPE, 1)
        lane = lax.broadcasted_iota(jnp.int32, (chunk, LANES), 1)
        nope1 = jnp.where(lane < ROPE, r1, r2).astype(jnp.bfloat16)
        cos, sin_up, sin_down = cos_ref[span, :], sin_up_ref[span, :], sin_down_ref[span, :]

        def turned(x):
            return (
                x * cos
                + pltpu.roll(x, ROPE // 2, 1) * sin_up
                + pltpu.roll(x, LANES - ROPE // 2, 1) * sin_down
            ).astype(jnp.bfloat16)

        queries = [
            jnp.concatenate([g0, turned(g1)], axis=1),
            jnp.concatenate([nope1, turned(r2)], axis=1),
        ]
        for h in range(2):
            scores = lax.dot_general(
                queries[h], keys[h], (((1,), (1,)), ((), ())), preferred_element_type=jnp.float32
            )
            scores = scores + bias_ref[span, :]
            top = jnp.max(scores, axis=1, keepdims=True)
            weights = jnp.exp2((scores - top) * SCALE2).astype(jnp.bfloat16)
            summed = jnp.dot(weights, values[h], preferred_element_type=jnp.float32)
            out_ref[span, h * VDIM : (h + 1) * VDIM] = (
                summed[:, :VDIM] / summed[:, VDIM : VDIM + 1]
            ).astype(out_ref.dtype)


def attend(queries, latents, up_weights, query_places, key_places):
    rows, key_count = queries.shape[0], latents.shape[0]
    pairs = queries.shape[1] // (2 * (NOPE + ROPE))
    angles = angles_of(query_places)
    cos, sin = jnp.cos(angles), jnp.sin(angles)
    zero, blank = jnp.zeros_like(cos), jnp.zeros((rows, LANES - ROPE), jnp.float32)
    cos_table = jnp.concatenate([cos, cos, blank], axis=1)
    sin_up = jnp.concatenate([zero, sin, blank], axis=1)
    sin_down = jnp.concatenate([-sin, zero, blank], axis=1)
    whole = lambda shape: pl.BlockSpec(shape, lambda i: (0, 0))
    return pl.pallas_call(
        attention_kernel,
        grid=(pairs,),
        out_shape=jax.ShapeDtypeStruct((rows, pairs * 2 * VDIM), jnp.bfloat16),
        in_specs=[
            pl.BlockSpec((rows, 2 * (NOPE + ROPE)), lambda i: (0, i)),
            whole((key_count, LATENT + LANES)),
            pl.BlockSpec((LATENT, 2 * (NOPE + VDIM)), lambda i: (0, i)),
            whole((rows, LANES)),
            whole((rows, LANES)),
            whole((rows, LANES)),
            whole((rows, 1)),
            whole((1, key_count)),
        ],
        out_specs=pl.BlockSpec((rows, 2 * VDIM), lambda i: (0, i)),
        scratch_shapes=[pltpu.VMEM((rows, key_count), jnp.float32)],
        compiler_params=pltpu.CompilerParams(vmem_limit_bytes=32 * 1024 * 1024),
        cost_estimate=pl.CostEstimate(
            flops=2 * pairs * 2 * key_count * (LATENT * 256 + rows * 512),
            bytes_accessed=2 * (queries.size + latents.size + up_weights.size),
            transcendentals=2 * pairs * rows * key_count,
        ),
    )(queries, latents, up_weights, cos_table, sin_up, sin_down, query_places[:, None], key_places[None, :])


def local(queries, latents, latent_gain, w_ukv, w_o, residual, block_order):
    order_row = block_order[0]
    ctx, tp = lax.axis_index("ctx"), lax.axis_index("tp")
    tp_count = lax.axis_size("tp")
    tok_dev = queries.shape[1]
    block_len = tok_dev // 2
    lat_rows = latents.shape[1]
    width = w_o.shape[2]
    swap = [(0, 1), (1, 0)]

    own_places = place_rows(order_row, (ctx * tp_count + tp) * lat_rows, lat_rows, block_len)
    latent_rows = latents[0].astype(jnp.float32)
    compressed = latent_rows[:, :LATENT]
    scale_rows = lax.rsqrt(jnp.mean(compressed * compressed, axis=-1, keepdims=True) + 1e-06)
    normed = (compressed * scale_rows * latent_gain[0][None, :]).astype(jnp.bfloat16)
    own_rope = rotate(latent_rows[:, LATENT:], own_places).astype(jnp.bfloat16)
    gathered, masks = gather_keys(jnp.concatenate([normed, own_rope], axis=-1))
    gathered = jnp.pad(gathered, ((0, 0), (0, LANES - ROPE)))
    key_places = jnp.concatenate(
        [
            place_rows(order_row, ((ctx ^ c) * tp_count + (tp ^ t)) * lat_rows, lat_rows, block_len)
            for c, t in masks
        ]
    )
    query_places = place_rows(order_row, ctx * tok_dev, tok_dev, block_len)
    attention = attend(queries[0], gathered, w_ukv[0], query_places, key_places)

    last = tp_count - 1
    rows_out = tok_dev // tp_count
    out_weights = w_o[0]

    def row_block(array, dest, lo, size):
        return lax.dynamic_slice(array, (dest * rows_out, lo), (rows_out, size))

    def spans(unit):
        count = UNIT_PIECES.get(unit, 1)
        return [(i * width // count, width // count) for i in range(count)]

    first_dest = jnp.where(tp == 0, last, 0)
    first_rows = lax.dynamic_slice(attention, (first_dest * rows_out, 0), (rows_out, attention.shape[1]))
    got = {}

    def send(hop, value):
        return lax.ppermute(value, "tp", [(hop, hop + 1), (last - hop, last - hop - 1)])

    for lo, size in spans(0):
        part = jnp.dot(first_rows, out_weights[:, lo : lo + size], preferred_element_type=jnp.float32)
        got[0, 0, lo] = send(0, part.astype(jnp.bfloat16))
    terms = jnp.dot(attention, out_weights, preferred_element_type=jnp.float32).astype(jnp.bfloat16)
    ahead = lax.ppermute(
        row_block(terms, jnp.where(tp == 0, 1, last - 1), 0, width), "pp", swap
    )
    for unit in range(1, tp_count - 1):
        for lo, size in spans(unit):
            if unit == tp_count - 2:
                value = ahead[:, lo : lo + size]
            else:
                value = row_block(terms, jnp.where(tp == 0, last - unit, unit), lo, size)
            got[0, unit, lo] = send(0, value)
    for hop in range(1, tp_count - 1):
        for unit in range(0, tp_count - 1 - hop):
            for lo, size in spans(unit):
                value = row_block(terms, jnp.where(tp == hop, last - unit, unit), lo, size)
                got[hop, unit, lo] = send(hop, value + got[hop - 1, unit, lo])

    def ended(hop):
        unit = tp_count - 2 - hop
        here = (tp == hop + 1) | (tp == last - hop - 1)
        whole = jnp.concatenate([got[hop, unit, lo] for lo, _ in spans(unit)], axis=1)
        return jnp.where(here, whole.astype(jnp.float32), 0.0)

    mixed = row_block(terms, tp, 0, width).astype(jnp.float32) + residual[0].astype(jnp.float32)
    for hop in range(1, tp_count - 1):
        mixed = mixed + ended(hop)
    handed = lax.ppermute(mixed.astype(jnp.bfloat16), "pp", swap)
    return (handed.astype(jnp.float32) + ended(0)).astype(jnp.bfloat16)[None]


def solution(mesh):
    in_specs = (
        P("pp", "ctx", "tp"),
        P("pp", ("ctx", "tp"), None),
        P("pp", None),
        P("pp", None, "tp"),
        P("pp", "tp", None),
        P("pp", ("ctx", "tp"), None),
        P("pp", None),
    )
    out_specs = P("pp", ("ctx", "tp"), None)
    return jax.shard_map(local, mesh=mesh, in_specs=in_specs, out_specs=out_specs, check_vma=False)
```

```python
import functools
import math

import jax
import jax.numpy as jnp
from jax import lax
from jax.experimental import pallas as pl
from jax.experimental.pallas import tpu as pltpu
from jax.sharding import PartitionSpec as P

NOPE = 128
ROPE = 64
VDIM = 128
LATENT = 512
LANES = 128

score_scale = 0.135
SCALE2 = score_scale * math.log2(math.e)

HEADS_STEP = 4
PIECES = 2


def angles_of(places):
    freqs = 10000.0 ** (-(jnp.arange(ROPE // 2).astype(jnp.float32) * 2.0 / ROPE))
    return places.astype(jnp.float32)[:, None] * freqs


def rotate(values, places):
    middle = values.shape[-1] // 2
    angles = angles_of(places)
    first_half = values[..., :middle]
    second_half = values[..., middle:]
    return jnp.concatenate(
        [
            first_half * jnp.cos(angles) - second_half * jnp.sin(angles),
            first_half * jnp.sin(angles) + second_half * jnp.cos(angles),
        ],
        axis=-1,
    )


def place_rows(order_row, first, count, block_len):
    row_ids = first + jnp.arange(count, dtype=jnp.int32)
    owners = row_ids // block_len
    table = jnp.arange(order_row.shape[0], dtype=jnp.int32)
    base = jnp.sum(jnp.where(owners[:, None] == table[None, :], order_row[None, :], 0), axis=1)
    return base * block_len + row_ids % block_len


def gather_keys(own_keys):
    tp_count, ctx_count = lax.axis_size("tp"), lax.axis_size("ctx")
    steps = [("tp", 1 << s) for s in range(tp_count.bit_length() - 1)]
    steps += [("ctx", 1 << s) for s in range(1, ctx_count.bit_length() - 1)]
    steps.append(("ctx", 1))
    halves, masks = (own_keys,), [(0, 0)]
    for axis, step in steps:
        held = halves[0] if len(halves) == 1 else jnp.concatenate(halves, axis=0)
        pairs = [(i, i ^ step) for i in range(lax.axis_size(axis))]
        halves = (held, lax.ppermute(held, axis, pairs))
        masks = masks + [
            (c ^ step, t) if axis == "ctx" else (c, t ^ step) for c, t in masks
        ]
    return halves, masks


def attention_kernel(
    slot_ref, q_ref, near_ref, far_ref, w_ref, cos_ref, sin_up_ref, sin_down_ref, qpos_ref, kpos_ref,
    out_ref, bias_ref,
):
    rows, half = q_ref.shape[0], near_ref.shape[0]
    heads = out_ref.shape[1] // VDIM
    blocks = slot_ref.shape[0]
    block = rows // blocks

    @pl.when(pl.program_id(0) == 0)
    def _():
        bias_ref[...] = jnp.where(kpos_ref[...] <= qpos_ref[...], 0.0, -1e30)

    produced, key_rope = [], []
    for part in (near_ref, far_ref):
        produced.append(
            jnp.dot(part[:, :LATENT], w_ref[...], preferred_element_type=jnp.float32).astype(jnp.bfloat16)
        )
        key_rope.append(
            jnp.concatenate([part[:, LATENT:], jnp.zeros((half, LANES - ROPE), jnp.bfloat16)], axis=1)
        )
    ones = jnp.ones((half, LANES), jnp.bfloat16)
    lane = lax.broadcasted_iota(jnp.int32, (rows, LANES), 1)

    def turned(x):
        return (
            x * cos_ref[...]
            + pltpu.roll(x, ROPE // 2, 1) * sin_up_ref[...]
            + pltpu.roll(x, LANES - ROPE // 2, 1) * sin_down_ref[...]
        ).astype(jnp.bfloat16)

    def query(h):
        base = (h // 2) * 2 * (NOPE + ROPE)
        middle = q_ref[:, base + LANES : base + 2 * LANES].astype(jnp.float32)
        if h % 2 == 0:
            return jnp.concatenate([q_ref[:, base : base + LANES], turned(middle)], axis=1)
        middle = pltpu.roll(middle, ROPE, 1)
        final = pltpu.roll(q_ref[:, base + 2 * LANES : base + 3 * LANES].astype(jnp.float32), ROPE, 1)
        nope = jnp.where(lane < ROPE, middle, final).astype(jnp.bfloat16)
        return jnp.concatenate([nope, turned(final)], axis=1)

    def scores(h):
        base = h * (NOPE + VDIM)
        q = query(h)
        return [
            lax.dot_general(
                q,
                jnp.concatenate([made[:, base : base + NOPE], rope], axis=1),
                (((1,), (1,)), ((), ())),
                preferred_element_type=jnp.float32,
            )
            for made, rope in zip(produced, key_rope)
        ]

    def weigh(found):
        found = [found[0] + bias_ref[:, :half], found[1] + bias_ref[:, half:]]
        top = jnp.max(jnp.maximum(found[0], found[1]), axis=1, keepdims=True)
        return [jnp.exp2((part - top) * SCALE2).astype(jnp.bfloat16) for part in found]

    def finish(h, weights):
        base = h * (NOPE + VDIM) + NOPE
        summed = sum(
            jnp.dot(
                part,
                jnp.concatenate([made[:, base : base + VDIM], ones], axis=1),
                preferred_element_type=jnp.float32,
            )
            for part, made in zip(weights, produced)
        )
        result = (summed[:, :VDIM] / summed[:, VDIM : VDIM + 1]).astype(out_ref.dtype)
        for dest in range(blocks):
            at = pl.multiple_of(slot_ref[dest] * block, block)
            out_ref[pl.ds(at, block), h * VDIM : (h + 1) * VDIM] = result[dest * block : (dest + 1) * block]

    found, weights = scores(0), None
    for h in range(heads):
        following = scores(h + 1) if h + 1 < heads else None
        now = weigh(found)
        if h > 0:
            finish(h - 1, weights)
        found, weights = following, now
    finish(heads - 1, weights)


def attend(queries, halves, up_weights, query_places, key_places, slots):
    rows, half = queries.shape[0], halves[0].shape[0]
    heads = queries.shape[1] // (NOPE + ROPE)
    angles = angles_of(query_places)
    cos, sin = jnp.cos(angles), jnp.sin(angles)
    zero, blank = jnp.zeros_like(cos), jnp.zeros((rows, LANES - ROPE), jnp.float32)
    cos_table = jnp.concatenate([cos, cos, blank], axis=1)
    sin_up = jnp.concatenate([zero, sin, blank], axis=1)
    sin_down = jnp.concatenate([-sin, zero, blank], axis=1)
    whole = lambda shape: pl.BlockSpec(shape, lambda i, s: (0, 0))
    along = lambda height, width: pl.BlockSpec((height, width), lambda i, s: (0, i))
    return pl.pallas_call(
        attention_kernel,
        out_shape=jax.ShapeDtypeStruct((rows, heads * VDIM), jnp.bfloat16),
        grid_spec=pltpu.PrefetchScalarGridSpec(
            num_scalar_prefetch=1,
            grid=(heads // HEADS_STEP,),
            in_specs=[
                along(rows, HEADS_STEP * (NOPE + ROPE)),
                whole(halves[0].shape),
                whole(halves[1].shape),
                along(LATENT, HEADS_STEP * (NOPE + VDIM)),
                whole((rows, LANES)),
                whole((rows, LANES)),
                whole((rows, LANES)),
                whole((rows, 1)),
                whole((1, 2 * half)),
            ],
            out_specs=along(rows, HEADS_STEP * VDIM),
            scratch_shapes=[pltpu.VMEM((rows, 2 * half), jnp.float32)],
        ),
        compiler_params=pltpu.CompilerParams(vmem_limit_bytes=56 * 1024 * 1024),
        cost_estimate=pl.CostEstimate(
            flops=4 * heads * half * (LATENT * 256 + rows * 512),
            bytes_accessed=2 * (queries.size + up_weights.size),
            transcendentals=2 * heads * rows * half,
        ),
    )(
        slots, queries, *halves, up_weights, cos_table, sin_up, sin_down,
        query_places[:, None], key_places[None, :],
    )


def project_kernel(x_ref, w_ref, *out_refs):
    block = out_refs[0].shape[0]
    made = jnp.dot(x_ref[...], w_ref[...], preferred_element_type=jnp.float32)
    for i, out in enumerate(out_refs):
        out[...] = made[i * block : (i + 1) * block].astype(out.dtype)


def project(rows, weights, lo, size, blocks):
    count, depth = rows.shape
    tile = max(t for t in range(LANES, 1024 + 1, LANES) if size % t == 0 and lo % t == 0)
    block = count // blocks
    return pl.pallas_call(
        project_kernel,
        grid=(size // tile,),
        out_shape=[jax.ShapeDtypeStruct((block, size), jnp.bfloat16)] * blocks,
        in_specs=[
            pl.BlockSpec((count, depth), lambda i: (0, 0)),
            pl.BlockSpec((depth, tile), lambda i: (0, i + lo // tile)),
        ],
        out_specs=[pl.BlockSpec((block, tile), lambda i: (0, i))] * blocks,
        compiler_params=pltpu.CompilerParams(vmem_limit_bytes=48 * 1024 * 1024),
        cost_estimate=pl.CostEstimate(
            flops=2 * count * depth * size, bytes_accessed=2 * depth * size, transcendentals=0
        ),
    )(rows, weights)


def add_kernel(always, count, flag_ref, *refs):
    total = refs[0][...].astype(jnp.float32)
    for ref in refs[1:always]:
        total = total + ref[...].astype(jnp.float32)
    for i, ref in enumerate(refs[always:count]):
        total = total + jnp.where(flag_ref[i] > 0, ref[...].astype(jnp.float32), 0.0)
    refs[-1][...] = total.astype(refs[-1].dtype)


def add_where(flags, values, flagged, earlier):
    count = len(values) + len(flagged)
    return pl.pallas_call(
        functools.partial(add_kernel, len(values), count),
        out_shape=jax.ShapeDtypeStruct(values[0].shape, jnp.bfloat16),
        in_specs=[pl.BlockSpec(memory_space=pltpu.SMEM)]
        + [pl.BlockSpec(memory_space=pltpu.VMEM)] * count
        + [pl.BlockSpec(memory_space=pl.ANY)] * len(earlier),
        out_specs=pl.BlockSpec(memory_space=pltpu.VMEM),
        compiler_params=pltpu.CompilerParams(vmem_limit_bytes=16 * 1024 * 1024),
    )(flags, *values, *flagged, *earlier)


def add_after(values, earlier):
    return add_where(jnp.ones((1,), jnp.int32), values, [], earlier)


def local(queries, latents, latent_gain, w_ukv, w_o, residual, block_order):
    order_row = block_order[0]
    ctx, tp = lax.axis_index("ctx"), lax.axis_index("tp")
    tp_count = lax.axis_size("tp")
    last = tp_count - 1
    tok_dev = queries.shape[1]
    block_len = tok_dev // 2
    lat_rows = latents.shape[1]
    width = w_o.shape[2]
    swap = [(0, 1), (1, 0)]

    own_places = place_rows(order_row, (ctx * tp_count + tp) * lat_rows, lat_rows, block_len)
    latent_rows = latents[0].astype(jnp.float32)
    compressed = latent_rows[:, :LATENT]
    scale_rows = lax.rsqrt(jnp.mean(compressed * compressed, axis=-1, keepdims=True) + 1e-06)
    normed = (compressed * scale_rows * latent_gain[0][None, :]).astype(jnp.bfloat16)
    own_rope = rotate(latent_rows[:, LATENT:], own_places).astype(jnp.bfloat16)
    halves, masks = gather_keys(jnp.concatenate([normed, own_rope], axis=-1))
    key_places = jnp.concatenate(
        [
            place_rows(order_row, ((ctx ^ c) * tp_count + (tp ^ t)) * lat_rows, lat_rows, block_len)
            for c, t in masks
        ]
    )
    query_places = place_rows(order_row, ctx * tok_dev, tok_dev, block_len)

    dests = jnp.arange(tp_count, dtype=jnp.int32)
    right_first = tp < tp_count // 2
    slots = jnp.where(
        dests == tp,
        last,
        jnp.where(
            right_first,
            jnp.where(dests > tp, last - dests, last - tp + dests),
            jnp.where(dests < tp, dests, tp + last - dests),
        ),
    )
    attention = attend(queries[0], halves, w_ukv[0], query_places, key_places, slots)

    def slot_of(hop, unit):
        return unit if 2 * hop < last else hop + unit

    def send(hop, value):
        return lax.ppermute(value, "tp", [(hop, hop + 1), (last - hop, last - hop - 1)])

    size = width // PIECES
    terms = [project(attention, w_o[0], i * size, size, tp_count) for i in range(PIECES)]
    got, ahead, sums = {}, {}, {}
    for i in range(PIECES):
        ahead[i] = lax.ppermute(terms[i][slot_of(0, last - 1)], "pp", swap)
        for unit in range(last):
            got[0, unit, i] = send(0, ahead[i] if unit == last - 1 else terms[i][slot_of(0, unit)])
    before = []
    for stage in range(1, last):
        for i in range(PIECES):
            sends = [(hop, stage - hop) for hop in range(1, stage + 1) if stage - hop < last - hop]
            arrived = [got[hop - 1, unit, i] for hop, unit in sends]
            if stage == 1:
                arrived.append(ahead[i])
            made = []
            for hop, unit in sends:
                own = terms[i][slot_of(hop, unit)]
                sums[hop, unit, i] = add_after([own, got[hop - 1, unit, i]], arrived + before)
                made.append(sums[hop, unit, i])
            for hop, unit in sends:
                got[hop, unit, i] = send(hop, sums[hop, unit, i])
            before = made

    outs = []
    for i in range(PIECES):
        kept = [terms[i][last], residual[0][:, i * size : (i + 1) * size]]
        ends = [(hop, last - 1 - hop) for hop in range(1, last)]
        flags = jnp.stack([(tp == hop + 1) | (tp == last - hop - 1) for hop, _ in ends]).astype(jnp.int32)
        arrived = [got[hop, unit, i] for hop, unit in ends]
        earlier = before + ([got[0, last - 1, i - 1]] if i > 0 else [])
        mixed = add_where(flags, kept, arrived, earlier)
        before = [mixed]
        handed = lax.ppermute(mixed, "pp", swap).astype(jnp.float32)
        here = (tp == 1) | (tp == last - 1)
        outs.append(handed + jnp.where(here, got[0, last - 1, i].astype(jnp.float32), 0.0))
    return jnp.concatenate(outs, axis=1).astype(jnp.bfloat16)[None]


def solution(mesh):
    in_specs = (
        P("pp", "ctx", "tp"),
        P("pp", ("ctx", "tp"), None),
        P("pp", None),
        P("pp", None, "tp"),
        P("pp", "tp", None),
        P("pp", ("ctx", "tp"), None),
        P("pp", None),
    )
    out_specs = P("pp", ("ctx", "tp"), None)
    return jax.shard_map(local, mesh=mesh, in_specs=in_specs, out_specs=out_specs, check_vma=False)
```

```python
import functools
import math

import jax
import jax.numpy as jnp
import numpy as np
from jax import lax
from jax.experimental import pallas as pl
from jax.experimental.pallas import tpu as pltpu
from jax.sharding import PartitionSpec as P

NOPE = 128
ROPE = 64
VDIM = 128
LATENT = 512
LANES = 128

score_scale = 0.135
SCALE2 = score_scale * math.log2(math.e)

HEADS_STEP = 4
MIB = 1024 * 1024
PREPARE_VMEM = 16 * MIB
PROJECT_VMEM = 24 * MIB
ATTEND_VMEM = 48 * MIB
ADD_VMEM = 8 * MIB
FINAL_FLOPS = 2 * 10**10
PIECES = 2


def row_places(order_ref, first, count, block_len):
    return order_ref[first // block_len] * block_len + first % block_len


def rope_tables(places):
    lane = lax.broadcasted_iota(jnp.int32, (places.shape[0], LANES), 1)
    angles = places.astype(jnp.float32) * lane_freqs()
    cos, sin = jnp.cos(angles), jnp.sin(angles)
    half = ROPE // 2
    return (
        jnp.where(lane < ROPE, cos, 0.0),
        jnp.where((lane >= half) & (lane < ROPE), sin, 0.0),
        jnp.where(lane < half, -sin, 0.0),
    )


def turned(x, cos, sin_up, sin_down):
    half = ROPE // 2
    return (
        x * cos + pltpu.roll(x, half, 1) * sin_up + pltpu.roll(x, LANES - half, 1) * sin_down
    ).astype(jnp.bfloat16)


def lane_freqs():
    half = ROPE // 2
    lane = lax.broadcasted_iota(jnp.int32, (1, LANES), 1) % half
    freqs = jnp.zeros((1, LANES), jnp.float32)
    for j in range(half):
        freqs = jnp.where(lane == j, np.float32(10000.0 ** (-2.0 * j / ROPE)), freqs)
    return freqs


def own_keys_kernel(block_len, order_ref, latent_ref, gain_ref, out_ref):
    rows = latent_ref.shape[0]
    first = (lax.axis_index("ctx") * lax.axis_size("tp") + lax.axis_index("tp")) * rows
    places = row_places(order_ref, first, rows, block_len) + lax.broadcasted_iota(jnp.int32, (rows, 1), 0)
    compressed = latent_ref[:, :LATENT].astype(jnp.float32)
    scale_rows = lax.rsqrt(jnp.mean(compressed * compressed, axis=-1, keepdims=True) + 1e-06)
    out_ref[:, :LATENT] = (compressed * scale_rows * gain_ref[...]).astype(jnp.bfloat16)
    rope = jnp.concatenate(
        [latent_ref[:, LATENT:].astype(jnp.float32), jnp.zeros((rows, LANES - ROPE), jnp.float32)], axis=1
    )
    out_ref[:, LATENT:] = turned(rope, *rope_tables(places))


def own_keys(order_row, latents, gain, block_len):
    return pl.pallas_call(
        functools.partial(own_keys_kernel, block_len),
        out_shape=jax.ShapeDtypeStruct((latents.shape[0], LATENT + LANES), jnp.bfloat16),
        in_specs=[pl.BlockSpec(memory_space=pltpu.SMEM)] + [pl.BlockSpec(memory_space=pltpu.VMEM)] * 2,
        out_specs=pl.BlockSpec(memory_space=pltpu.VMEM),
        compiler_params=pltpu.CompilerParams(vmem_limit_bytes=60 * MIB),
    )(order_row, latents, gain)


def join_kernel(count, *refs):
    at = 0
    for ref in refs[:count]:
        refs[-1][at : at + ref.shape[0], :] = ref[...]
        at += ref.shape[0]


def join_after(arrays, earlier):
    rows = sum(array.shape[0] for array in arrays)
    return pl.pallas_call(
        functools.partial(join_kernel, len(arrays)),
        out_shape=jax.ShapeDtypeStruct((rows, arrays[0].shape[1]), arrays[0].dtype),
        in_specs=[pl.BlockSpec(memory_space=pltpu.VMEM)] * len(arrays)
        + [pl.BlockSpec(memory_space=pl.ANY)] * len(earlier),
        out_specs=pl.BlockSpec(memory_space=pltpu.VMEM),
        compiler_params=pltpu.CompilerParams(vmem_limit_bytes=16 * 1024 * 1024),
    )(*arrays, *earlier)


def gather_masks():
    masks = [(0, 0)]
    for s in range(lax.axis_size("tp").bit_length() - 1):
        masks = masks + [(c, t ^ (1 << s)) for c, t in masks]
    for s in list(range(1, lax.axis_size("ctx").bit_length() - 1)) + [0]:
        masks = masks + [(c ^ (1 << s), t) for c, t in masks]
    return masks


def gather_keys(own, earlier):
    tp_count, ctx_count = lax.axis_size("tp"), lax.axis_size("ctx")

    def traded(value, axis, step):
        return lax.ppermute(value, axis, [(i, i ^ step) for i in range(lax.axis_size(axis))])

    pieces = [own]
    for s in range(tp_count.bit_length() - 1):
        held = own if s == 0 else join_after(pieces, [])
        pieces = [held, traded(held, "tp", 1 << s)]
    pieces[-1] = join_after(pieces[-1:], earlier)
    for s in list(range(1, ctx_count.bit_length() - 1)) + [0]:
        pieces = pieces + [traded(piece, "ctx", 1 << s) for piece in pieces]
    return pieces


def prepare_kernel(block_len, key_rows, masks, order_ref, q_hbm, out_ref, bias_ref, q_ref, semaphore):
    rows = q_ref.shape[0]
    fetch = pltpu.make_async_copy(q_hbm, q_ref, semaphore)
    fetch.start()
    tp_count = lax.axis_size("tp")
    ctx, tp = lax.axis_index("ctx"), lax.axis_index("tp")
    row = lax.broadcasted_iota(jnp.int32, (rows, 1), 0)
    places = jnp.zeros((rows, 1), jnp.int32)
    for b in range(rows // block_len):
        base = row_places(order_ref, ctx * rows + b * block_len, block_len, block_len)
        places = jnp.where(row // block_len == b, base + row % block_len, places)
    lane = lax.broadcasted_iota(jnp.int32, (1, LANES), 1)
    group = LANES // key_rows
    for g in range(len(masks) // group):
        keys = jnp.zeros((1, LANES), jnp.int32)
        for j in range(group):
            c, t = masks[g * group + j]
            base = row_places(order_ref, ((ctx ^ c) * tp_count + (tp ^ t)) * key_rows, key_rows, block_len)
            keys = jnp.where(lane // key_rows == j, base + lane % key_rows, keys)
        bias_ref[:, g * LANES : (g + 1) * LANES] = jnp.where(keys <= places, 0.0, -1e30)
    tables = rope_tables(places)
    lane = lax.broadcasted_iota(jnp.int32, (rows, LANES), 1)
    fetch.wait()
    per_step = HEADS_STEP // 2
    for pair in range(q_ref.shape[1] // (3 * LANES)):
        step, base, to = pair // per_step, pair * 3 * LANES, pair % per_step * 4 * LANES
        middle = q_ref[:, base + LANES : base + 2 * LANES].astype(jnp.float32)
        out_ref[step, :, to : to + LANES] = q_ref[:, base : base + LANES]
        out_ref[step, :, to + LANES : to + 2 * LANES] = turned(middle, *tables)
        middle = pltpu.roll(middle, ROPE, 1)
        final = pltpu.roll(q_ref[:, base + 2 * LANES : base + 3 * LANES].astype(jnp.float32), ROPE, 1)
        nope = jnp.where(lane < ROPE, middle, final).astype(jnp.bfloat16)
        out_ref[step, :, to + 2 * LANES : to + 3 * LANES] = nope
        out_ref[step, :, to + 3 * LANES : to + 4 * LANES] = turned(final, *tables)


def prepare(order_row, queries, key_rows, masks, block_len):
    rows = queries.shape[0]
    heads = queries.shape[1] // (NOPE + ROPE)
    key_count = key_rows * len(masks)
    return pl.pallas_call(
        functools.partial(prepare_kernel, block_len, key_rows, masks),
        out_shape=[
            jax.ShapeDtypeStruct((heads // HEADS_STEP, rows, HEADS_STEP * 2 * LANES), jnp.bfloat16),
            jax.ShapeDtypeStruct((rows, key_count), jnp.float32),
        ],
        in_specs=[
            pl.BlockSpec(memory_space=pltpu.SMEM),
            pl.BlockSpec(memory_space=pltpu.HBM),
        ],
        out_specs=[pl.BlockSpec(memory_space=pltpu.VMEM)] * 2,
        scratch_shapes=[pltpu.VMEM(queries.shape, queries.dtype), pltpu.SemaphoreType.DMA],
        compiler_params=pltpu.CompilerParams(vmem_limit_bytes=PREPARE_VMEM),
        cost_estimate=pl.CostEstimate(flops=20 * queries.size, bytes_accessed=6 * queries.size, transcendentals=0),
    )(order_row, queries)


def slot_of_dest(dest):
    tp, last = lax.axis_index("tp"), lax.axis_size("tp") - 1
    right_first = jnp.where(dest > tp, last - dest, last - tp + dest)
    left_first = jnp.where(dest < tp, dest, tp + last - dest)
    return jnp.where(dest == tp, last, jnp.where(2 * tp <= last, right_first, left_first))


def attention_kernel(piece_count, steps, *refs):
    q_ref, bias_ref, w_ref, out_w_ref = refs[:4]
    piece_refs = refs[4 : 4 + piece_count]
    rest_refs = refs[4 + piece_count :]
    attention_ref, term_refs = rest_refs[0], rest_refs[1:-4]
    keys_ref, held_ref, columns_ref, semaphores = rest_refs[-4:]
    step = pl.program_id(0)
    block = q_ref.shape[1] // len(term_refs)
    tiles, _, tile = columns_ref.shape

    def column_copy(i):
        return pltpu.make_async_copy(
            out_w_ref.at[:, pl.ds(i * tile, tile)], columns_ref.at[i], semaphores.at[i]
        )

    @pl.when(step == 0)
    def _():
        for i in range(tiles):
            column_copy(i).start()
        at = 0
        for ref in piece_refs:
            keys_ref[at : at + ref.shape[0], :] = ref[...]
            at += ref.shape[0]

    @pl.when(step < steps)
    def _():
        attend_heads(step, q_ref, bias_ref, w_ref, keys_ref, held_ref, len(term_refs))

    @pl.when(step == steps)
    def _():
        wide = held_ref.shape[2]
        for i in range(steps):
            attention_ref[:, i * wide : (i + 1) * wide] = held_ref[i]
        for i in range(tiles):
            column_copy(i).wait()

    @pl.when(step >= steps)
    def _():
        made = jnp.dot(attention_ref[...], columns_ref[step - steps], preferred_element_type=jnp.float32)
        for i, out in enumerate(term_refs):
            out[...] = made[i * block : (i + 1) * block].astype(out.dtype)


def attend_heads(step, q_ref, bias_ref, w_ref, keys_ref, held_ref, blocks):
    half = keys_ref.shape[0] // 2
    block = q_ref.shape[1] // blocks
    produced = [
        jnp.dot(
            keys_ref[part * half : (part + 1) * half, :LATENT], w_ref[...], preferred_element_type=jnp.float32
        ).astype(jnp.bfloat16)
        for part in range(2)
    ]
    key_rope = [keys_ref[part * half : (part + 1) * half, LATENT:] for part in range(2)]
    ones = jnp.ones((half, LANES), jnp.bfloat16)

    def scores(h):
        base = h * (NOPE + VDIM)
        return [
            lax.dot_general(
                q_ref[step, :, h * 2 * LANES : (h + 1) * 2 * LANES],
                jnp.concatenate([made[:, base : base + NOPE], rope], axis=1),
                (((1,), (1,)), ((), ())),
                preferred_element_type=jnp.float32,
            )
            for made, rope in zip(produced, key_rope)
        ]

    def weigh(found):
        found = [found[0] + bias_ref[:, :half], found[1] + bias_ref[:, half:]]
        top = jnp.max(jnp.maximum(found[0], found[1]), axis=1, keepdims=True)
        return [jnp.exp2((part - top) * SCALE2).astype(jnp.bfloat16) for part in found]

    def finish(h, weights):
        base = h * (NOPE + VDIM) + NOPE
        summed = sum(
            jnp.dot(
                part,
                jnp.concatenate([made[:, base : base + VDIM], ones], axis=1),
                preferred_element_type=jnp.float32,
            )
            for part, made in zip(weights, produced)
        )
        result = (summed[:, :VDIM] / summed[:, VDIM : VDIM + 1]).astype(held_ref.dtype)
        for dest in range(blocks):
            at = pl.multiple_of(slot_of_dest(dest) * block, block)
            held_ref[step, pl.ds(at, block), h * VDIM : (h + 1) * VDIM] = result[dest * block : (dest + 1) * block]

    found, weights = scores(0), None
    for h in range(HEADS_STEP):
        following = scores(h + 1) if h + 1 < HEADS_STEP else None
        now = weigh(found)
        if h > 0:
            finish(h - 1, weights)
        found, weights = following, now
    finish(HEADS_STEP - 1, weights)


def column_tile(lo, size, most):
    return max(t for t in range(LANES, most + 1, LANES) if size % t == 0 and lo % t == 0)


def attend(queries, bias, pieces, up_weights, out_weights, size, blocks):
    rows, key_count = bias.shape
    steps = queries.shape[0]
    heads = steps * HEADS_STEP
    depth = heads * VDIM
    tile = column_tile(0, size, 1024)
    head_step = lambda i: jnp.minimum(i, steps - 1)
    column_step = lambda i: jnp.maximum(i - steps, 0)
    whole = lambda shape: pl.BlockSpec(shape, lambda i: (0, 0))
    return pl.pallas_call(
        functools.partial(attention_kernel, len(pieces), steps),
        grid=(steps + size // tile,),
        out_shape=[
            jax.ShapeDtypeStruct((rows, depth), jnp.bfloat16),
        ]
        + [jax.ShapeDtypeStruct((rows // blocks, size), jnp.bfloat16)] * blocks,
        in_specs=[
            pl.BlockSpec(memory_space=pltpu.VMEM),
            pl.BlockSpec(memory_space=pltpu.VMEM),
            pl.BlockSpec((LATENT, HEADS_STEP * (NOPE + VDIM)), lambda i: (0, head_step(i))),
            pl.BlockSpec(memory_space=pltpu.HBM),
        ]
        + [pl.BlockSpec(memory_space=pltpu.VMEM)] * len(pieces),
        out_specs=[pl.BlockSpec(memory_space=pltpu.VMEM)]
        + [pl.BlockSpec((rows // blocks, tile), lambda i: (0, column_step(i)))] * blocks,
        scratch_shapes=[
            pltpu.VMEM((key_count, LATENT + LANES), jnp.bfloat16),
            pltpu.VMEM((steps, rows, HEADS_STEP * VDIM), jnp.bfloat16),
            pltpu.VMEM((size // tile, depth, tile), jnp.bfloat16),
            pltpu.SemaphoreType.DMA((size // tile,)),
        ],
        compiler_params=pltpu.CompilerParams(vmem_limit_bytes=ATTEND_VMEM),
        cost_estimate=pl.CostEstimate(
            flops=2 * heads * key_count * (LATENT * 256 + rows * 512) + 2 * rows * depth * size,
            bytes_accessed=2 * (queries.size + up_weights.size + depth * size),
            transcendentals=heads * rows * key_count,
        ),
    )(queries, bias, up_weights, out_weights, *pieces)


def project_kernel(x_ref, upper_ref, lower_ref, *out_refs):
    block, half = out_refs[0].shape[0], upper_ref.shape[0]
    made = jnp.dot(x_ref[:, :half], upper_ref[...], preferred_element_type=jnp.float32)
    made = made + jnp.dot(x_ref[:, half:], lower_ref[...], preferred_element_type=jnp.float32)
    for i, out in enumerate(out_refs):
        out[...] = made[i * block : (i + 1) * block].astype(out.dtype)


def project(rows, weights, lo, size, blocks):
    count, depth = rows.shape
    tile = column_tile(lo, size, 1024)
    block = count // blocks
    return pl.pallas_call(
        project_kernel,
        grid=(size // tile,),
        out_shape=[jax.ShapeDtypeStruct((block, size), jnp.bfloat16)] * blocks,
        in_specs=[
            pl.BlockSpec((count, depth), lambda i: (0, 0)),
            pl.BlockSpec((depth // 2, tile), lambda i: (0, i + lo // tile)),
            pl.BlockSpec((depth // 2, tile), lambda i: (1, i + lo // tile)),
        ],
        out_specs=[pl.BlockSpec((block, tile), lambda i: (0, i))] * blocks,
        compiler_params=pltpu.CompilerParams(vmem_limit_bytes=PROJECT_VMEM),
        cost_estimate=pl.CostEstimate(
            flops=2 * count * depth * size, bytes_accessed=2 * depth * size, transcendentals=0
        ),
    )(rows, weights, weights)


def total_of(refs, flag_ref, always):
    total = jnp.zeros(refs[0].shape, jnp.float32)
    for i, ref in enumerate(refs):
        value = ref[...].astype(jnp.float32)
        total = total + (value if i < always else jnp.where(flag_ref[i - always] > 0, value, 0.0))
    return total.astype(jnp.bfloat16)


def add_kernel(count, *refs):
    refs[-1][...] = total_of(refs[:count], None, count)


def add_after(values, earlier):
    return pl.pallas_call(
        functools.partial(add_kernel, len(values)),
        out_shape=jax.ShapeDtypeStruct(values[0].shape, jnp.bfloat16),
        in_specs=[pl.BlockSpec(memory_space=pltpu.VMEM)] * len(values)
        + [pl.BlockSpec(memory_space=pl.ANY)] * len(earlier),
        out_specs=pl.BlockSpec(memory_space=pltpu.VMEM),
        compiler_params=pltpu.CompilerParams(vmem_limit_bytes=ADD_VMEM),
    )(*values, *earlier)


def pair_kernel(own_ref, rest_ref, unit_ref, out_ref):
    rows = own_ref.shape[0]
    out_ref[:rows, :] = total_of([own_ref, rest_ref], None, 2)
    out_ref[rows:, :] = unit_ref[...]


def pair_up(own, rest, unit):
    rows, size = own.shape
    return pl.pallas_call(
        pair_kernel,
        out_shape=jax.ShapeDtypeStruct((2 * rows, size), jnp.bfloat16),
        in_specs=[pl.BlockSpec(memory_space=pltpu.VMEM)] * 3,
        out_specs=pl.BlockSpec(memory_space=pltpu.VMEM),
        compiler_params=pltpu.CompilerParams(vmem_limit_bytes=ADD_VMEM),
    )(own, rest, unit)


def finish_kernel(count, flag_ref, pair_ref, *refs):
    rows = refs[-1].shape[0]
    refs[-1][...] = total_of([pair_ref.at[:rows, :], *refs[:count]], flag_ref, 1)


def finish(flags, pair, flagged, piece, pieces, before):
    rows, size = flagged[0].shape
    operands = [flags, pair, *flagged] + before
    return pl.pallas_call(
        functools.partial(finish_kernel, len(flagged)),
        grid=(1,),
        out_shape=jax.ShapeDtypeStruct((rows, size * pieces), jnp.bfloat16),
        in_specs=[pl.BlockSpec(memory_space=pltpu.SMEM)]
        + [pl.BlockSpec(memory_space=pltpu.VMEM)] * (1 + len(flagged))
        + [pl.BlockSpec(memory_space=pl.ANY)] * len(before),
        out_specs=pl.BlockSpec((rows, size), lambda i: (0, piece)),
        input_output_aliases={len(operands) - 1: 0} if before else {},
        compiler_params=pltpu.CompilerParams(vmem_limit_bytes=ADD_VMEM),
        cost_estimate=pl.CostEstimate(flops=FINAL_FLOPS, bytes_accessed=0, transcendentals=0),
    )(*operands)


def local(queries, latents, latent_gain, w_ukv, w_o, residual, block_order):
    tp = lax.axis_index("tp")
    tp_count = lax.axis_size("tp")
    last = tp_count - 1
    tok_dev, lat_rows, width = queries.shape[1], latents.shape[1], w_o.shape[2]
    order_row = block_order[0]
    block_len = tok_dev * lax.axis_size("ctx") // order_row.shape[0]
    size = width // PIECES

    turned_queries, bias = prepare(order_row, queries[0], lat_rows, gather_masks(), block_len)
    pieces = gather_keys(own_keys(order_row, latents[0], latent_gain, block_len), [turned_queries, bias])
    attention, *first_terms = attend(turned_queries, bias, pieces, w_ukv[0], w_o[0], size, tp_count)

    def slot_of(hop, unit):
        return unit if 2 * hop < last else hop + unit

    def send(hop, value, across):
        steps = [(hop, hop + 1), (last - hop, last - hop - 1)]
        if not across:
            return lax.ppermute(value, "tp", steps)
        return lax.ppermute(
            value, ("tp", "pp"), [(2 * i + p, 2 * j + 1 - p) for i, j in steps for p in range(2)]
        )

    def flags_of(*conditions):
        return jnp.stack(conditions).astype(jnp.int32)

    terms = [first_terms] + [project(attention, w_o[0], i * size, size, tp_count) for i in range(1, PIECES)]
    got, ahead = {}, {}
    for i in range(PIECES):
        for unit in range(last - 1):
            got[0, unit, i] = send(0, terms[i][slot_of(0, unit)], False)
        rest = residual[0][:, i * size : (i + 1) * size]
        both = pair_up(terms[i][last], rest, terms[i][slot_of(0, last - 1)])
        ahead[i] = lax.ppermute(both, "pp", [(0, 1), (1, 0)])
        got[0, last - 1, i] = send(0, ahead[i][rest.shape[0] :], False)
    before = []
    for stage in range(1, last):
        for i in range(PIECES):
            for hop in range(stage, 0, -1):
                unit = stage - hop
                if unit >= last - hop:
                    continue
                if (stage, hop, i) == (2, 1, 0):
                    before = before + [ahead[0]]
                summed = add_after([terms[i][slot_of(hop, unit)], got[hop - 1, unit, i]], before)
                before = [summed]
                got[hop, unit, i] = send(hop, summed, unit == last - 1 - hop)

    flags = flags_of(*[(tp == hop + 1) | (tp == last - hop - 1) for hop in range(last)])
    out = []
    for i in range(PIECES):
        ended = [got[hop, last - 1 - hop, i] for hop in range(last)]
        out = [finish(flags, ahead[i], ended, i, PIECES, out)]
    return out[0][None]


def solution(mesh):
    in_specs = (
        P("pp", "ctx", "tp"),
        P("pp", ("ctx", "tp"), None),
        P("pp", None),
        P("pp", None, "tp"),
        P("pp", "tp", None),
        P("pp", ("ctx", "tp"), None),
        P("pp", None),
    )
    out_specs = P("pp", ("ctx", "tp"), None)
    return jax.shard_map(local, mesh=mesh, in_specs=in_specs, out_specs=out_specs, check_vma=False)
```

```python
import functools
import math

import jax
import jax.numpy as jnp
import numpy as np
from jax import lax
from jax.experimental import pallas as pl
from jax.experimental.pallas import tpu as pltpu
from jax.sharding import PartitionSpec as P

NOPE = 128
ROPE = 64
VDIM = 128
LATENT = 512
LANES = 128

score_scale = 0.135
SCALE2 = score_scale * math.log2(math.e)

HEADS_STEP = 8
MIB = 1024 * 1024
PREPARE_VMEM = 16 * MIB
PROJECT_VMEM = 24 * MIB
ATTEND_VMEM = 48 * MIB
ADD_VMEM = 8 * MIB
FINAL_FLOPS = 10**10
FIRST_SHARE = 50
PIECES = 2
TILE = 896


def row_places(order_ref, first, count, block_len):
    return order_ref[first // block_len] * block_len + first % block_len


def rope_tables(places):
    lane = lax.broadcasted_iota(jnp.int32, (places.shape[0], LANES), 1)
    angles = places.astype(jnp.float32) * lane_freqs()
    cos, sin = jnp.cos(angles), jnp.sin(angles)
    half = ROPE // 2
    return (
        jnp.where(lane < ROPE, cos, 0.0),
        jnp.where((lane >= half) & (lane < ROPE), sin, 0.0),
        jnp.where(lane < half, -sin, 0.0),
    )


def turned(x, cos, sin_up, sin_down):
    half = ROPE // 2
    return (
        x * cos + pltpu.roll(x, half, 1) * sin_up + pltpu.roll(x, LANES - half, 1) * sin_down
    ).astype(jnp.bfloat16)


def lane_freqs():
    half = ROPE // 2
    lane = lax.broadcasted_iota(jnp.int32, (1, LANES), 1) % half
    freqs = jnp.zeros((1, LANES), jnp.float32)
    for j in range(half):
        freqs = jnp.where(lane == j, np.float32(10000.0 ** (-2.0 * j / ROPE)), freqs)
    return freqs


def own_keys_kernel(block_len, order_ref, latent_ref, gain_ref, out_ref):
    rows = latent_ref.shape[0]
    first = (lax.axis_index("ctx") * lax.axis_size("tp") + lax.axis_index("tp")) * rows
    places = row_places(order_ref, first, rows, block_len) + lax.broadcasted_iota(jnp.int32, (rows, 1), 0)
    compressed = latent_ref[:, :LATENT].astype(jnp.float32)
    scale_rows = lax.rsqrt(jnp.mean(compressed * compressed, axis=-1, keepdims=True) + 1e-06)
    out_ref[:, :LATENT] = (compressed * scale_rows * gain_ref[...]).astype(jnp.bfloat16)
    rope = jnp.concatenate(
        [latent_ref[:, LATENT:].astype(jnp.float32), jnp.zeros((rows, LANES - ROPE), jnp.float32)], axis=1
    )
    out_ref[:, LATENT:] = turned(rope, *rope_tables(places))


def own_keys(order_row, latents, gain, block_len):
    return pl.pallas_call(
        functools.partial(own_keys_kernel, block_len),
        out_shape=pltpu.VMEM((latents.shape[0], LATENT + LANES), jnp.bfloat16),
        in_specs=[pl.BlockSpec(memory_space=pltpu.SMEM)] + [pl.BlockSpec(memory_space=pltpu.VMEM)] * 2,
        out_specs=pl.BlockSpec(memory_space=pltpu.VMEM),
        compiler_params=pltpu.CompilerParams(vmem_limit_bytes=60 * MIB),
    )(order_row, latents, gain)


def join_kernel(count, *refs):
    at = 0
    for ref in refs[:count]:
        refs[-1][at : at + ref.shape[0], :] = ref[...]
        at += ref.shape[0]


def join_after(arrays, earlier):
    rows = sum(array.shape[0] for array in arrays)
    return pl.pallas_call(
        functools.partial(join_kernel, len(arrays)),
        out_shape=jax.ShapeDtypeStruct((rows, arrays[0].shape[1]), arrays[0].dtype),
        in_specs=[pl.BlockSpec(memory_space=pltpu.VMEM)] * len(arrays)
        + [pl.BlockSpec(memory_space=pl.ANY)] * len(earlier),
        out_specs=pl.BlockSpec(memory_space=pltpu.VMEM),
        compiler_params=pltpu.CompilerParams(vmem_limit_bytes=16 * 1024 * 1024),
    )(*arrays, *earlier)


def gather_masks():
    masks = [(0, 0)]
    for s in range(lax.axis_size("tp").bit_length() - 1):
        masks = masks + [(c, t ^ (1 << s)) for c, t in masks]
    for s in list(range(1, lax.axis_size("ctx").bit_length() - 1)) + [0]:
        masks = masks + [(c ^ (1 << s), t) for c, t in masks]
    return masks


def gather_keys(own, earlier):
    tp_count, ctx_count = lax.axis_size("tp"), lax.axis_size("ctx")

    def traded(value, axis, step):
        return lax.ppermute(value, axis, [(i, i ^ step) for i in range(lax.axis_size(axis))])

    pieces = [own]
    for s in range(tp_count.bit_length() - 1):
        held = own if s == 0 else join_after(pieces, [])
        pieces = [held, traded(held, "tp", 1 << s)]
    pieces[-1] = join_after(pieces[-1:], earlier)
    for s in list(range(1, ctx_count.bit_length() - 1)) + [0]:
        pieces = pieces + [traded(piece, "ctx", 1 << s) for piece in pieces]
    return pieces


def prepare_kernel(block_len, key_rows, masks, order_ref, q_hbm, out_ref, bias_ref, q_ref, semaphore):
    rows = q_ref.shape[0]
    fetch = pltpu.make_async_copy(q_hbm, q_ref, semaphore)
    fetch.start()
    tp_count = lax.axis_size("tp")
    ctx, tp = lax.axis_index("ctx"), lax.axis_index("tp")
    row = lax.broadcasted_iota(jnp.int32, (rows, 1), 0)
    places = jnp.zeros((rows, 1), jnp.int32)
    for b in range(rows // block_len):
        base = row_places(order_ref, ctx * rows + b * block_len, block_len, block_len)
        places = jnp.where(row // block_len == b, base + row % block_len, places)
    lane = lax.broadcasted_iota(jnp.int32, (1, LANES), 1)
    group = LANES // key_rows
    for g in range(len(masks) // group):
        keys = jnp.zeros((1, LANES), jnp.int32)
        for j in range(group):
            c, t = masks[g * group + j]
            base = row_places(order_ref, ((ctx ^ c) * tp_count + (tp ^ t)) * key_rows, key_rows, block_len)
            keys = jnp.where(lane // key_rows == j, base + lane % key_rows, keys)
        bias_ref[:, g * LANES : (g + 1) * LANES] = jnp.where(keys <= places, 0.0, -1e30)
    tables = rope_tables(places)
    lane = lax.broadcasted_iota(jnp.int32, (rows, LANES), 1)
    fetch.wait()
    per_step = HEADS_STEP // 2
    for pair in range(q_ref.shape[1] // (3 * LANES)):
        step, base, to = pair // per_step, pair * 3 * LANES, pair % per_step * 4 * LANES
        middle = q_ref[:, base + LANES : base + 2 * LANES].astype(jnp.float32)
        out_ref[step, :, to : to + LANES] = q_ref[:, base : base + LANES]
        out_ref[step, :, to + LANES : to + 2 * LANES] = turned(middle, *tables)
        middle = pltpu.roll(middle, ROPE, 1)
        final = pltpu.roll(q_ref[:, base + 2 * LANES : base + 3 * LANES].astype(jnp.float32), ROPE, 1)
        nope = jnp.where(lane < ROPE, middle, final).astype(jnp.bfloat16)
        out_ref[step, :, to + 2 * LANES : to + 3 * LANES] = nope
        out_ref[step, :, to + 3 * LANES : to + 4 * LANES] = turned(final, *tables)


def prepare(order_row, queries, key_rows, masks, block_len):
    rows = queries.shape[0]
    heads = queries.shape[1] // (NOPE + ROPE)
    key_count = key_rows * len(masks)
    return pl.pallas_call(
        functools.partial(prepare_kernel, block_len, key_rows, masks),
        out_shape=[
            jax.ShapeDtypeStruct((heads // HEADS_STEP, rows, HEADS_STEP * 2 * LANES), jnp.bfloat16),
            jax.ShapeDtypeStruct((rows, key_count), jnp.float32),
        ],
        in_specs=[
            pl.BlockSpec(memory_space=pltpu.SMEM),
            pl.BlockSpec(memory_space=pltpu.HBM),
        ],
        out_specs=[pl.BlockSpec(memory_space=pltpu.VMEM)] * 2,
        scratch_shapes=[pltpu.VMEM(queries.shape, queries.dtype), pltpu.SemaphoreType.DMA],
        compiler_params=pltpu.CompilerParams(vmem_limit_bytes=PREPARE_VMEM),
        cost_estimate=pl.CostEstimate(flops=20 * queries.size, bytes_accessed=6 * queries.size, transcendentals=0),
    )(order_row, queries)


def slot_of_dest(dest):
    tp, last = lax.axis_index("tp"), lax.axis_size("tp") - 1
    right_first = jnp.where(dest > tp, last - dest, last - tp + dest)
    left_first = jnp.where(dest < tp, dest, tp + last - dest)
    return jnp.where(dest == tp, last, jnp.where(2 * tp <= last, right_first, left_first))


def attention_kernel(piece_count, steps, *refs):
    q_ref, bias_ref, w_ref, out_w_ref = refs[:4]
    piece_refs = refs[4 : 4 + piece_count]
    rest_refs = refs[4 + piece_count :]
    attention_ref, term_refs = rest_refs[0], rest_refs[1:-4]
    keys_ref, held_ref, columns_ref, semaphores = rest_refs[-4:]
    step = pl.program_id(0)
    block = q_ref.shape[1] // len(term_refs)
    tiles, _, tile = columns_ref.shape

    def column_copy(i):
        return pltpu.make_async_copy(
            out_w_ref.at[:, pl.ds(i * tile, tile)], columns_ref.at[i], semaphores.at[i]
        )

    @pl.when(step == 0)
    def _():
        for i in range(tiles):
            column_copy(i).start()
        at = 0
        for ref in piece_refs:
            keys_ref[at : at + ref.shape[0], :] = ref[...]
            at += ref.shape[0]

    @pl.when(step < steps)
    def _():
        attend_heads(step, q_ref, bias_ref, w_ref, keys_ref, held_ref, len(term_refs))

    @pl.when(step == steps)
    def _():
        wide = held_ref.shape[2]
        for i in range(steps):
            attention_ref[:, i * wide : (i + 1) * wide] = held_ref[i]
        for i in range(tiles):
            column_copy(i).wait()

    @pl.when(step >= steps)
    def _():
        made = jnp.dot(attention_ref[...], columns_ref[step - steps], preferred_element_type=jnp.float32)
        for i, out in enumerate(term_refs):
            out[...] = made[i * block : (i + 1) * block].astype(out.dtype)


def attend_heads(step, q_ref, bias_ref, w_ref, keys_ref, held_ref, blocks):
    half = keys_ref.shape[0] // 2
    block = q_ref.shape[1] // blocks
    produced = [
        jnp.dot(
            keys_ref[part * half : (part + 1) * half, :LATENT], w_ref[...], preferred_element_type=jnp.float32
        ).astype(jnp.bfloat16)
        for part in range(2)
    ]
    key_rope = [keys_ref[part * half : (part + 1) * half, LATENT:] for part in range(2)]
    ones = jnp.ones((half, LANES), jnp.bfloat16)

    def scores(h):
        base = h * (NOPE + VDIM)
        return [
            lax.dot_general(
                q_ref[step, :, h * 2 * LANES : (h + 1) * 2 * LANES],
                jnp.concatenate([made[:, base : base + NOPE], rope], axis=1),
                (((1,), (1,)), ((), ())),
                preferred_element_type=jnp.float32,
            )
            for made, rope in zip(produced, key_rope)
        ]

    def weigh(found):
        found = [found[0] + bias_ref[:, :half], found[1] + bias_ref[:, half:]]
        top = jnp.max(jnp.maximum(found[0], found[1]), axis=1, keepdims=True)
        return [jnp.exp2((part - top) * SCALE2).astype(jnp.bfloat16) for part in found]

    def finish(h, weights):
        base = h * (NOPE + VDIM) + NOPE
        summed = sum(
            jnp.dot(
                part,
                jnp.concatenate([made[:, base : base + VDIM], ones], axis=1),
                preferred_element_type=jnp.float32,
            )
            for part, made in zip(weights, produced)
        )
        result = (summed[:, :VDIM] / summed[:, VDIM : VDIM + 1]).astype(held_ref.dtype)
        for dest in range(blocks):
            at = pl.multiple_of(slot_of_dest(dest) * block, block)
            held_ref[step, pl.ds(at, block), h * VDIM : (h + 1) * VDIM] = result[dest * block : (dest + 1) * block]

    found, weights = scores(0), None
    for h in range(HEADS_STEP):
        following = scores(h + 1) if h + 1 < HEADS_STEP else None
        now = weigh(found)
        if h > 0:
            finish(h - 1, weights)
        found, weights = following, now
    finish(HEADS_STEP - 1, weights)


def column_tile(lo, size, most):
    return max(t for t in range(LANES, most + 1, LANES) if size % t == 0 and lo % t == 0)


def attend(queries, bias, pieces, up_weights, out_weights, size, blocks):
    rows, key_count = bias.shape
    steps = queries.shape[0]
    heads = steps * HEADS_STEP
    depth = heads * VDIM
    tile = column_tile(0, size, TILE)
    head_step = lambda i: jnp.minimum(i, steps - 1)
    column_step = lambda i: jnp.maximum(i - steps, 0)
    whole = lambda shape: pl.BlockSpec(shape, lambda i: (0, 0))
    return pl.pallas_call(
        functools.partial(attention_kernel, len(pieces), steps),
        grid=(steps + size // tile,),
        out_shape=[
            jax.ShapeDtypeStruct((rows, depth), jnp.bfloat16),
        ]
        + [jax.ShapeDtypeStruct((rows // blocks, size), jnp.bfloat16)] * blocks,
        in_specs=[
            pl.BlockSpec(memory_space=pltpu.VMEM),
            pl.BlockSpec(memory_space=pltpu.VMEM),
            pl.BlockSpec((LATENT, HEADS_STEP * (NOPE + VDIM)), lambda i: (0, head_step(i))),
            pl.BlockSpec(memory_space=pltpu.HBM),
        ]
        + [pl.BlockSpec(memory_space=pltpu.VMEM)] * len(pieces),
        out_specs=[pl.BlockSpec(memory_space=pltpu.VMEM)]
        + [pl.BlockSpec((rows // blocks, tile), lambda i: (0, column_step(i)))] * blocks,
        scratch_shapes=[
            pltpu.VMEM((key_count, LATENT + LANES), jnp.bfloat16),
            pltpu.VMEM((steps, rows, HEADS_STEP * VDIM), jnp.bfloat16),
            pltpu.VMEM((size // tile, depth, tile), jnp.bfloat16),
            pltpu.SemaphoreType.DMA((size // tile,)),
        ],
        compiler_params=pltpu.CompilerParams(vmem_limit_bytes=ATTEND_VMEM),
        cost_estimate=pl.CostEstimate(
            flops=2 * heads * key_count * (LATENT * 256 + rows * 512) + 2 * rows * depth * size,
            bytes_accessed=2 * (queries.size + up_weights.size + depth * size),
            transcendentals=heads * rows * key_count,
        ),
    )(queries, bias, up_weights, out_weights, *pieces)


def project_kernel(x_ref, upper_ref, lower_ref, *out_refs):
    block, half = out_refs[0].shape[0], upper_ref.shape[0]
    made = jnp.dot(x_ref[:, :half], upper_ref[...], preferred_element_type=jnp.float32)
    made = made + jnp.dot(x_ref[:, half:], lower_ref[...], preferred_element_type=jnp.float32)
    for i, out in enumerate(out_refs):
        out[...] = made[i * block : (i + 1) * block].astype(out.dtype)


def project(rows, weights, lo, size, blocks):
    count, depth = rows.shape
    tile = column_tile(lo, size, TILE)
    block = count // blocks
    return pl.pallas_call(
        project_kernel,
        grid=(size // tile,),
        out_shape=[jax.ShapeDtypeStruct((block, size), jnp.bfloat16)] * blocks,
        in_specs=[
            pl.BlockSpec((count, depth), lambda i: (0, 0)),
            pl.BlockSpec((depth // 2, tile), lambda i: (0, i + lo // tile)),
            pl.BlockSpec((depth // 2, tile), lambda i: (1, i + lo // tile)),
        ],
        out_specs=[pl.BlockSpec((block, tile), lambda i: (0, i))] * blocks,
        compiler_params=pltpu.CompilerParams(vmem_limit_bytes=PROJECT_VMEM),
        cost_estimate=pl.CostEstimate(
            flops=2 * count * depth * size, bytes_accessed=2 * depth * size, transcendentals=0
        ),
    )(rows, weights, weights)


def total_of(refs, flag_ref, always):
    total = jnp.zeros(refs[0].shape, jnp.float32)
    for i, ref in enumerate(refs):
        value = ref[...].astype(jnp.float32)
        total = total + (value if i < always else jnp.where(flag_ref[i - always] > 0, value, 0.0))
    return total.astype(jnp.bfloat16)


def add_kernel(count, *refs):
    refs[-1][...] = total_of(refs[:count], None, count)


def add_after(values, earlier):
    return pl.pallas_call(
        functools.partial(add_kernel, len(values)),
        out_shape=jax.ShapeDtypeStruct(values[0].shape, jnp.bfloat16),
        in_specs=[pl.BlockSpec(memory_space=pltpu.VMEM)] * len(values)
        + [pl.BlockSpec(memory_space=pl.ANY)] * len(earlier),
        out_specs=pl.BlockSpec(memory_space=pltpu.VMEM),
        compiler_params=pltpu.CompilerParams(vmem_limit_bytes=ADD_VMEM),
    )(*values, *earlier)


def pair_kernel(own_ref, rest_ref, unit_ref, out_ref):
    rows = own_ref.shape[0]
    out_ref[:rows, :] = total_of([own_ref, rest_ref], None, 2)
    out_ref[rows:, :] = unit_ref[...]


def pair_up(own, rest, unit):
    rows, size = own.shape
    return pl.pallas_call(
        pair_kernel,
        out_shape=jax.ShapeDtypeStruct((2 * rows, size), jnp.bfloat16),
        in_specs=[pl.BlockSpec(memory_space=pltpu.VMEM)] * 3,
        out_specs=pl.BlockSpec(memory_space=pltpu.VMEM),
        compiler_params=pltpu.CompilerParams(vmem_limit_bytes=ADD_VMEM),
    )(own, rest, unit)


def finish_kernel(lo, count, flag_ref, pair_ref, *refs):
    out_hbm, held_ref, semaphore = refs[-3:]
    rows, size = held_ref.shape
    held_ref[...] = total_of([pair_ref.at[:rows, :], *refs[:count]], flag_ref, 1)
    copy = pltpu.make_async_copy(held_ref, out_hbm.at[:, pl.ds(lo, size)], semaphore)
    copy.start()
    copy.wait()


def finish(flags, pair, flagged, lo, width, before):
    rows, size = flagged[0].shape
    operands = [flags, pair, *flagged] + before
    return pl.pallas_call(
        functools.partial(finish_kernel, lo, len(flagged)),
        out_shape=jax.ShapeDtypeStruct((rows, width), jnp.bfloat16),
        in_specs=[pl.BlockSpec(memory_space=pltpu.SMEM)]
        + [pl.BlockSpec(memory_space=pltpu.VMEM)] * (1 + len(flagged))
        + [pl.BlockSpec(memory_space=pl.ANY)] * len(before),
        out_specs=pl.BlockSpec(memory_space=pl.ANY),
        scratch_shapes=[pltpu.VMEM((rows, size), jnp.bfloat16), pltpu.SemaphoreType.DMA],
        input_output_aliases={len(operands) - 1: 0} if before else {},
        compiler_params=pltpu.CompilerParams(vmem_limit_bytes=ADD_VMEM),
        cost_estimate=pl.CostEstimate(flops=FINAL_FLOPS, bytes_accessed=0, transcendentals=0),
    )(*operands)


def local(queries, latents, latent_gain, w_ukv, w_o, residual, block_order):
    tp = lax.axis_index("tp")
    tp_count = lax.axis_size("tp")
    last = tp_count - 1
    tok_dev, lat_rows, width = queries.shape[1], latents.shape[1], w_o.shape[2]
    order_row = block_order[0]
    block_len = tok_dev * lax.axis_size("ctx") // order_row.shape[0]
    tile = column_tile(0, width, TILE)
    first_size = -(-width * FIRST_SHARE // (100 * tile)) * tile
    spans = [(0, first_size), (first_size, width - first_size)]

    turned_queries, bias = prepare(order_row, queries[0], lat_rows, gather_masks(), block_len)
    pieces = gather_keys(own_keys(order_row, latents[0], latent_gain, block_len), [turned_queries, bias])
    attention, *first_terms = attend(turned_queries, bias, pieces, w_ukv[0], w_o[0], first_size, tp_count)

    def slot_of(hop, unit):
        return unit if 2 * hop < last else hop + unit

    def send(hop, value, across):
        steps = [(hop, hop + 1), (last - hop, last - hop - 1)]
        if not across:
            return lax.ppermute(value, "tp", steps)
        return lax.ppermute(
            value, ("tp", "pp"), [(2 * i + p, 2 * j + 1 - p) for i, j in steps for p in range(2)]
        )

    def flags_of(*conditions):
        return jnp.stack(conditions).astype(jnp.int32)

    terms = [first_terms] + [project(attention, w_o[0], *span, tp_count) for span in spans[1:]]
    got, ahead = {}, {}
    for i in range(PIECES):
        for unit in range(last - 1):
            got[0, unit, i] = send(0, terms[i][slot_of(0, unit)], False)
        lo, size = spans[i]
        rest = residual[0][:, lo : lo + size]
        both = pair_up(terms[i][last], rest, terms[i][slot_of(0, last - 1)])
        ahead[i] = lax.ppermute(both, "pp", [(0, 1), (1, 0)])
        got[0, last - 1, i] = send(0, ahead[i][rest.shape[0] :], False)
    before = []
    for stage in range(1, last):
        for i in range(PIECES):
            for hop in range(stage, 0, -1):
                unit = stage - hop
                if unit >= last - hop:
                    continue
                if (stage, hop, i) == (2, 1, 0):
                    before = before + [ahead[0]]
                summed = add_after([terms[i][slot_of(hop, unit)], got[hop - 1, unit, i]], before)
                before = [summed]
                got[hop, unit, i] = send(hop, summed, unit == last - 1 - hop)

    flags = flags_of(*[(tp == hop + 1) | (tp == last - hop - 1) for hop in range(last)])
    out = []
    for i in range(PIECES):
        ended = [got[hop, last - 1 - hop, i] for hop in range(last)]
        out = [finish(flags, ahead[i], ended, spans[i][0], width, out)]
    return out[0][None]


def solution(mesh):
    in_specs = (
        P("pp", "ctx", "tp"),
        P("pp", ("ctx", "tp"), None),
        P("pp", None),
        P("pp", None, "tp"),
        P("pp", "tp", None),
        P("pp", ("ctx", "tp"), None),
        P("pp", None),
    )
    out_specs = P("pp", ("ctx", "tp"), None)
    return jax.shard_map(local, mesh=mesh, in_specs=in_specs, out_specs=out_specs, check_vma=False)
```

```python
import functools
import math

import jax
import jax.numpy as jnp
import numpy as np
from jax import lax
from jax.experimental import pallas as pl
from jax.experimental.pallas import tpu as pltpu
from jax.sharding import PartitionSpec as P

NOPE = 128
ROPE = 64
VDIM = 128
LATENT = 512
LANES = 128

score_scale = 0.135
SCALE2 = score_scale * math.log2(math.e)

HEADS_STEP = 8
MIB = 1024 * 1024
PREPARE_VMEM = 16 * MIB
PROJECT_VMEM = 24 * MIB
ATTEND_VMEM = 48 * MIB
ADD_VMEM = 8 * MIB
FINAL_FLOPS = 10**10
FIRST_SHARE = 50
PIECES = 2
TILE = 896


def row_places(order_ref, first, count, block_len):
    return order_ref[first // block_len] * block_len + first % block_len


def rope_tables(places):
    lane = lax.broadcasted_iota(jnp.int32, (places.shape[0], LANES), 1)
    angles = places.astype(jnp.float32) * lane_freqs()
    cos, sin = jnp.cos(angles), jnp.sin(angles)
    half = ROPE // 2
    return (
        jnp.where(lane < ROPE, cos, 0.0),
        jnp.where((lane >= half) & (lane < ROPE), sin, 0.0),
        jnp.where(lane < half, -sin, 0.0),
    )


def turned(x, cos, sin_up, sin_down):
    half = ROPE // 2
    return (
        x * cos + pltpu.roll(x, half, 1) * sin_up + pltpu.roll(x, LANES - half, 1) * sin_down
    ).astype(jnp.bfloat16)


def lane_freqs():
    half = ROPE // 2
    lane = lax.broadcasted_iota(jnp.int32, (1, LANES), 1) % half
    freqs = jnp.zeros((1, LANES), jnp.float32)
    for j in range(half):
        freqs = jnp.where(lane == j, np.float32(10000.0 ** (-2.0 * j / ROPE)), freqs)
    return freqs


def own_keys_kernel(block_len, order_ref, latent_ref, gain_ref, out_ref):
    rows = latent_ref.shape[0]
    first = (lax.axis_index("ctx") * lax.axis_size("tp") + lax.axis_index("tp")) * rows
    places = row_places(order_ref, first, rows, block_len) + lax.broadcasted_iota(jnp.int32, (rows, 1), 0)
    compressed = latent_ref[:, :LATENT].astype(jnp.float32)
    scale_rows = lax.rsqrt(jnp.mean(compressed * compressed, axis=-1, keepdims=True) + 1e-06)
    out_ref[:, :LATENT] = (compressed * scale_rows * gain_ref[...]).astype(jnp.bfloat16)
    rope = jnp.concatenate(
        [latent_ref[:, LATENT:].astype(jnp.float32), jnp.zeros((rows, LANES - ROPE), jnp.float32)], axis=1
    )
    out_ref[:, LATENT:] = turned(rope, *rope_tables(places))


def own_keys(order_row, latents, gain, block_len):
    return pl.pallas_call(
        functools.partial(own_keys_kernel, block_len),
        out_shape=pltpu.VMEM((latents.shape[0], LATENT + LANES), jnp.bfloat16),
        in_specs=[pl.BlockSpec(memory_space=pltpu.SMEM)] + [pl.BlockSpec(memory_space=pltpu.VMEM)] * 2,
        out_specs=pl.BlockSpec(memory_space=pltpu.VMEM),
        compiler_params=pltpu.CompilerParams(vmem_limit_bytes=60 * MIB),
    )(order_row, latents, gain)


def join_kernel(count, *refs):
    at = 0
    for ref in refs[:count]:
        refs[-1][at : at + ref.shape[0], :] = ref[...]
        at += ref.shape[0]


def join_after(arrays, earlier):
    rows = sum(array.shape[0] for array in arrays)
    return pl.pallas_call(
        functools.partial(join_kernel, len(arrays)),
        out_shape=jax.ShapeDtypeStruct((rows, arrays[0].shape[1]), arrays[0].dtype),
        in_specs=[pl.BlockSpec(memory_space=pltpu.VMEM)] * len(arrays)
        + [pl.BlockSpec(memory_space=pl.ANY)] * len(earlier),
        out_specs=pl.BlockSpec(memory_space=pltpu.VMEM),
        compiler_params=pltpu.CompilerParams(vmem_limit_bytes=16 * 1024 * 1024),
    )(*arrays, *earlier)


def gather_masks():
    masks = [(0, 0)]
    for s in range(lax.axis_size("tp").bit_length() - 1):
        masks = masks + [(c, t ^ (1 << s)) for c, t in masks]
    for s in list(range(1, lax.axis_size("ctx").bit_length() - 1)) + [0]:
        masks = masks + [(c ^ (1 << s), t) for c, t in masks]
    return masks


def gather_keys(own, earlier):
    tp_count, ctx_count = lax.axis_size("tp"), lax.axis_size("ctx")

    def traded(value, axis, step):
        return lax.ppermute(value, axis, [(i, i ^ step) for i in range(lax.axis_size(axis))])

    pieces = [own]
    for s in range(tp_count.bit_length() - 1):
        held = own if s == 0 else join_after(pieces, [])
        pieces = [held, traded(held, "tp", 1 << s)]
    pieces[-1] = join_after(pieces[-1:], earlier)
    for s in list(range(1, ctx_count.bit_length() - 1)) + [0]:
        pieces = pieces + [traded(piece, "ctx", 1 << s) for piece in pieces]
    return pieces


def prepare_kernel(block_len, key_rows, masks, order_ref, q_hbm, out_ref, bias_ref, q_ref, semaphore):
    rows = q_ref.shape[0]
    fetch = pltpu.make_async_copy(q_hbm, q_ref, semaphore)
    fetch.start()
    tp_count = lax.axis_size("tp")
    ctx, tp = lax.axis_index("ctx"), lax.axis_index("tp")
    row = lax.broadcasted_iota(jnp.int32, (rows, 1), 0)
    places = jnp.zeros((rows, 1), jnp.int32)
    for b in range(rows // block_len):
        base = row_places(order_ref, ctx * rows + b * block_len, block_len, block_len)
        places = jnp.where(row // block_len == b, base + row % block_len, places)
    lane = lax.broadcasted_iota(jnp.int32, (1, LANES), 1)
    group = LANES // key_rows
    for g in range(len(masks) // group):
        keys = jnp.zeros((1, LANES), jnp.int32)
        for j in range(group):
            c, t = masks[g * group + j]
            base = row_places(order_ref, ((ctx ^ c) * tp_count + (tp ^ t)) * key_rows, key_rows, block_len)
            keys = jnp.where(lane // key_rows == j, base + lane % key_rows, keys)
        bias_ref[:, g * LANES : (g + 1) * LANES] = jnp.where(keys <= places, 0.0, -1e30)
    tables = rope_tables(places)
    lane = lax.broadcasted_iota(jnp.int32, (rows, LANES), 1)
    fetch.wait()
    per_step = HEADS_STEP // 2
    for pair in range(q_ref.shape[1] // (3 * LANES)):
        step, base, to = pair // per_step, pair * 3 * LANES, pair % per_step * 4 * LANES
        middle = q_ref[:, base + LANES : base + 2 * LANES].astype(jnp.float32)
        out_ref[step, :, to : to + LANES] = q_ref[:, base : base + LANES]
        out_ref[step, :, to + LANES : to + 2 * LANES] = turned(middle, *tables)
        middle = pltpu.roll(middle, ROPE, 1)
        final = pltpu.roll(q_ref[:, base + 2 * LANES : base + 3 * LANES].astype(jnp.float32), ROPE, 1)
        nope = jnp.where(lane < ROPE, middle, final).astype(jnp.bfloat16)
        out_ref[step, :, to + 2 * LANES : to + 3 * LANES] = nope
        out_ref[step, :, to + 3 * LANES : to + 4 * LANES] = turned(final, *tables)


def prepare(order_row, queries, key_rows, masks, block_len):
    rows = queries.shape[0]
    heads = queries.shape[1] // (NOPE + ROPE)
    key_count = key_rows * len(masks)
    return pl.pallas_call(
        functools.partial(prepare_kernel, block_len, key_rows, masks),
        out_shape=[
            jax.ShapeDtypeStruct((heads // HEADS_STEP, rows, HEADS_STEP * 2 * LANES), jnp.bfloat16),
            jax.ShapeDtypeStruct((rows, key_count), jnp.float32),
        ],
        in_specs=[
            pl.BlockSpec(memory_space=pltpu.SMEM),
            pl.BlockSpec(memory_space=pltpu.HBM),
        ],
        out_specs=[pl.BlockSpec(memory_space=pltpu.VMEM)] * 2,
        scratch_shapes=[pltpu.VMEM(queries.shape, queries.dtype), pltpu.SemaphoreType.DMA],
        compiler_params=pltpu.CompilerParams(vmem_limit_bytes=PREPARE_VMEM),
        cost_estimate=pl.CostEstimate(flops=20 * queries.size, bytes_accessed=6 * queries.size, transcendentals=0),
    )(order_row, queries)


def slot_of_dest(dest):
    tp, last = lax.axis_index("tp"), lax.axis_size("tp") - 1
    right_first = jnp.where(dest > tp, last - dest, last - tp + dest)
    left_first = jnp.where(dest < tp, dest, tp + last - dest)
    return jnp.where(dest == tp, last, jnp.where(2 * tp <= last, right_first, left_first))


def attention_kernel(piece_count, steps, *refs):
    q_ref, bias_ref, w_ref, out_w_ref = refs[:4]
    piece_refs = refs[4 : 4 + piece_count]
    rest_refs = refs[4 + piece_count :]
    attention_ref, term_refs = rest_refs[0], rest_refs[1:-4]
    keys_ref, held_ref, columns_ref, semaphores = rest_refs[-4:]
    step = pl.program_id(0)
    block = q_ref.shape[1] // len(term_refs)
    tiles, _, tile = columns_ref.shape

    def column_copy(i):
        return pltpu.make_async_copy(
            out_w_ref.at[:, pl.ds(i * tile, tile)], columns_ref.at[i], semaphores.at[i]
        )

    @pl.when(step == 0)
    def _():
        for i in range(tiles):
            column_copy(i).start()
        at = 0
        for ref in piece_refs:
            keys_ref[at : at + ref.shape[0], :] = ref[...]
            at += ref.shape[0]

    @pl.when(step < steps)
    def _():
        attend_heads(step, q_ref, bias_ref, w_ref, keys_ref, held_ref, len(term_refs))

    @pl.when(step == steps)
    def _():
        wide = held_ref.shape[2]
        for i in range(steps):
            attention_ref[:, i * wide : (i + 1) * wide] = held_ref[i]
        for i in range(tiles):
            column_copy(i).wait()

    @pl.when(step >= steps)
    def _():
        made = jnp.dot(attention_ref[...], columns_ref[step - steps], preferred_element_type=jnp.float32)
        for i, out in enumerate(term_refs):
            out[...] = made[i * block : (i + 1) * block].astype(out.dtype)


def attend_heads(step, q_ref, bias_ref, w_ref, keys_ref, held_ref, blocks):
    half = keys_ref.shape[0] // 2
    block = q_ref.shape[1] // blocks
    produced = [
        jnp.dot(
            keys_ref[part * half : (part + 1) * half, :LATENT], w_ref[...], preferred_element_type=jnp.float32
        ).astype(jnp.bfloat16)
        for part in range(2)
    ]
    key_rope = [keys_ref[part * half : (part + 1) * half, LATENT:] for part in range(2)]
    ones = jnp.ones((half, LANES), jnp.bfloat16)

    def scores(h):
        base = h * (NOPE + VDIM)
        return [
            lax.dot_general(
                q_ref[step, :, h * 2 * LANES : (h + 1) * 2 * LANES],
                jnp.concatenate([made[:, base : base + NOPE], rope], axis=1),
                (((1,), (1,)), ((), ())),
                preferred_element_type=jnp.float32,
            )
            for made, rope in zip(produced, key_rope)
        ]

    def weigh(found):
        found = [found[0] + bias_ref[:, :half], found[1] + bias_ref[:, half:]]
        top = jnp.max(jnp.maximum(found[0], found[1]), axis=1, keepdims=True)
        return [jnp.exp2((part - top) * SCALE2).astype(jnp.bfloat16) for part in found]

    def finish(h, weights):
        base = h * (NOPE + VDIM) + NOPE
        summed = sum(
            jnp.dot(
                part,
                jnp.concatenate([made[:, base : base + VDIM], ones], axis=1),
                preferred_element_type=jnp.float32,
            )
            for part, made in zip(weights, produced)
        )
        result = (summed[:, :VDIM] / summed[:, VDIM : VDIM + 1]).astype(held_ref.dtype)
        for dest in range(blocks):
            at = pl.multiple_of(slot_of_dest(dest) * block, block)
            held_ref[step, pl.ds(at, block), h * VDIM : (h + 1) * VDIM] = result[dest * block : (dest + 1) * block]

    found, weights = scores(0), None
    for h in range(HEADS_STEP):
        following = scores(h + 1) if h + 1 < HEADS_STEP else None
        now = weigh(found)
        if h > 0:
            finish(h - 1, weights)
        found, weights = following, now
    finish(HEADS_STEP - 1, weights)


def column_tile(lo, size, most):
    return max(t for t in range(LANES, most + 1, LANES) if size % t == 0 and lo % t == 0)


def attend(queries, bias, pieces, up_weights, out_weights, size, blocks):
    rows, key_count = bias.shape
    steps = queries.shape[0]
    heads = steps * HEADS_STEP
    depth = heads * VDIM
    tile = column_tile(0, size, 4 * TILE)
    head_step = lambda i: jnp.minimum(i, steps - 1)
    column_step = lambda i: jnp.maximum(i - steps, 0)
    whole = lambda shape: pl.BlockSpec(shape, lambda i: (0, 0))
    return pl.pallas_call(
        functools.partial(attention_kernel, len(pieces), steps),
        grid=(steps + size // tile,),
        out_shape=[
            jax.ShapeDtypeStruct((rows, depth), jnp.bfloat16),
        ]
        + [jax.ShapeDtypeStruct((rows // blocks, size), jnp.bfloat16)] * blocks,
        in_specs=[
            pl.BlockSpec(memory_space=pltpu.VMEM),
            pl.BlockSpec(memory_space=pltpu.VMEM),
            pl.BlockSpec((LATENT, HEADS_STEP * (NOPE + VDIM)), lambda i: (0, head_step(i))),
            pl.BlockSpec(memory_space=pltpu.HBM),
        ]
        + [pl.BlockSpec(memory_space=pltpu.VMEM)] * len(pieces),
        out_specs=[pl.BlockSpec(memory_space=pltpu.VMEM)]
        + [pl.BlockSpec((rows // blocks, tile), lambda i: (0, column_step(i)))] * blocks,
        scratch_shapes=[
            pltpu.VMEM((key_count, LATENT + LANES), jnp.bfloat16),
            pltpu.VMEM((steps, rows, HEADS_STEP * VDIM), jnp.bfloat16),
            pltpu.VMEM((size // tile, depth, tile), jnp.bfloat16),
            pltpu.SemaphoreType.DMA((size // tile,)),
        ],
        compiler_params=pltpu.CompilerParams(vmem_limit_bytes=ATTEND_VMEM),
        cost_estimate=pl.CostEstimate(
            flops=2 * heads * key_count * (LATENT * 256 + rows * 512) + 2 * rows * depth * size,
            bytes_accessed=2 * (queries.size + up_weights.size + depth * size),
            transcendentals=heads * rows * key_count,
        ),
    )(queries, bias, up_weights, out_weights, *pieces)


def project_kernel(x_ref, upper_ref, lower_ref, *out_refs):
    block, half = out_refs[0].shape[0], upper_ref.shape[0]
    made = jnp.dot(x_ref[:, :half], upper_ref[...], preferred_element_type=jnp.float32)
    made = made + jnp.dot(x_ref[:, half:], lower_ref[...], preferred_element_type=jnp.float32)
    for i, out in enumerate(out_refs):
        out[...] = made[i * block : (i + 1) * block].astype(out.dtype)


def project(rows, weights, lo, size, blocks):
    count, depth = rows.shape
    tile = column_tile(lo, size, TILE)
    block = count // blocks
    return pl.pallas_call(
        project_kernel,
        grid=(size // tile,),
        out_shape=[jax.ShapeDtypeStruct((block, size), jnp.bfloat16)] * blocks,
        in_specs=[
            pl.BlockSpec((count, depth), lambda i: (0, 0)),
            pl.BlockSpec((depth // 2, tile), lambda i: (0, i + lo // tile)),
            pl.BlockSpec((depth // 2, tile), lambda i: (1, i + lo // tile)),
        ],
        out_specs=[pl.BlockSpec((block, tile), lambda i: (0, i))] * blocks,
        compiler_params=pltpu.CompilerParams(vmem_limit_bytes=PROJECT_VMEM),
        cost_estimate=pl.CostEstimate(
            flops=2 * count * depth * size, bytes_accessed=2 * depth * size, transcendentals=0
        ),
    )(rows, weights, weights)


def total_of(refs, flag_ref, always):
    total = jnp.zeros(refs[0].shape, jnp.float32)
    for i, ref in enumerate(refs):
        value = ref[...].astype(jnp.float32)
        total = total + (value if i < always else jnp.where(flag_ref[i - always] > 0, value, 0.0))
    return total.astype(jnp.bfloat16)


def add_kernel(count, *refs):
    refs[-1][...] = total_of(refs[:count], None, count)


def add_after(values, earlier):
    return pl.pallas_call(
        functools.partial(add_kernel, len(values)),
        out_shape=jax.ShapeDtypeStruct(values[0].shape, jnp.bfloat16),
        in_specs=[pl.BlockSpec(memory_space=pltpu.VMEM)] * len(values)
        + [pl.BlockSpec(memory_space=pl.ANY)] * len(earlier),
        out_specs=pl.BlockSpec(memory_space=pltpu.VMEM),
        compiler_params=pltpu.CompilerParams(vmem_limit_bytes=ADD_VMEM),
    )(*values, *earlier)


def pair_kernel(own_ref, rest_ref, unit_ref, out_ref):
    rows = own_ref.shape[0]
    out_ref[:rows, :] = total_of([own_ref, rest_ref], None, 2)
    out_ref[rows:, :] = unit_ref[...]


def pair_up(own, rest, unit):
    rows, size = own.shape
    return pl.pallas_call(
        pair_kernel,
        out_shape=jax.ShapeDtypeStruct((2 * rows, size), jnp.bfloat16),
        in_specs=[pl.BlockSpec(memory_space=pltpu.VMEM)] * 3,
        out_specs=pl.BlockSpec(memory_space=pltpu.VMEM),
        compiler_params=pltpu.CompilerParams(vmem_limit_bytes=ADD_VMEM),
    )(own, rest, unit)


def finish_kernel(lo, count, flag_ref, pair_ref, *refs):
    out_hbm, held_ref, semaphore = refs[-3:]
    rows, size = held_ref.shape
    held_ref[...] = total_of([pair_ref.at[:rows, :], *refs[:count]], flag_ref, 1)
    copy = pltpu.make_async_copy(held_ref, out_hbm.at[:, pl.ds(lo, size)], semaphore)
    copy.start()
    copy.wait()


def finish(flags, pair, flagged, lo, width, before):
    rows, size = flagged[0].shape
    operands = [flags, pair, *flagged] + before
    return pl.pallas_call(
        functools.partial(finish_kernel, lo, len(flagged)),
        out_shape=jax.ShapeDtypeStruct((rows, width), jnp.bfloat16),
        in_specs=[pl.BlockSpec(memory_space=pltpu.SMEM)]
        + [pl.BlockSpec(memory_space=pltpu.VMEM)] * (1 + len(flagged))
        + [pl.BlockSpec(memory_space=pl.ANY)] * len(before),
        out_specs=pl.BlockSpec(memory_space=pl.ANY),
        scratch_shapes=[pltpu.VMEM((rows, size), jnp.bfloat16), pltpu.SemaphoreType.DMA],
        input_output_aliases={len(operands) - 1: 0} if before else {},
        compiler_params=pltpu.CompilerParams(vmem_limit_bytes=ADD_VMEM),
        cost_estimate=pl.CostEstimate(flops=FINAL_FLOPS, bytes_accessed=0, transcendentals=0),
    )(*operands)


def local(queries, latents, latent_gain, w_ukv, w_o, residual, block_order):
    tp = lax.axis_index("tp")
    tp_count = lax.axis_size("tp")
    last = tp_count - 1
    tok_dev, lat_rows, width = queries.shape[1], latents.shape[1], w_o.shape[2]
    order_row = block_order[0]
    block_len = tok_dev * lax.axis_size("ctx") // order_row.shape[0]
    tile = column_tile(0, width, TILE)
    first_size = -(-width * FIRST_SHARE // (100 * tile)) * tile
    spans = [(0, first_size), (first_size, width - first_size)]

    turned_queries, bias = prepare(order_row, queries[0], lat_rows, gather_masks(), block_len)
    pieces = gather_keys(own_keys(order_row, latents[0], latent_gain, block_len), [turned_queries, bias])
    attention, *first_terms = attend(turned_queries, bias, pieces, w_ukv[0], w_o[0], first_size, tp_count)

    def slot_of(hop, unit):
        return unit if 2 * hop < last else hop + unit

    def send(hop, value, across):
        steps = [(hop, hop + 1), (last - hop, last - hop - 1)]
        if not across:
            return lax.ppermute(value, "tp", steps)
        return lax.ppermute(
            value, ("tp", "pp"), [(2 * i + p, 2 * j + 1 - p) for i, j in steps for p in range(2)]
        )

    def flags_of(*conditions):
        return jnp.stack(conditions).astype(jnp.int32)

    terms = [first_terms] + [project(attention, w_o[0], *span, tp_count) for span in spans[1:]]
    got, ahead = {}, {}
    for i in range(PIECES):
        for unit in range(last - 1):
            got[0, unit, i] = send(0, terms[i][slot_of(0, unit)], False)
        lo, size = spans[i]
        rest = residual[0][:, lo : lo + size]
        both = pair_up(terms[i][last], rest, terms[i][slot_of(0, last - 1)])
        ahead[i] = lax.ppermute(both, "pp", [(0, 1), (1, 0)])
        got[0, last - 1, i] = send(0, ahead[i][rest.shape[0] :], False)
    before = []
    for stage in range(1, last):
        for i in range(PIECES):
            for hop in range(stage, 0, -1):
                unit = stage - hop
                if unit >= last - hop:
                    continue
                if (stage, hop, i) == (2, 1, 0):
                    before = before + [ahead[0]]
                summed = add_after([terms[i][slot_of(hop, unit)], got[hop - 1, unit, i]], before)
                before = [summed]
                got[hop, unit, i] = send(hop, summed, unit == last - 1 - hop)

    flags = flags_of(*[(tp == hop + 1) | (tp == last - hop - 1) for hop in range(last)])
    out = []
    for i in range(PIECES):
        ended = [got[hop, last - 1 - hop, i] for hop in range(last)]
        out = [finish(flags, ahead[i], ended, spans[i][0], width, out)]
    return out[0][None]


def solution(mesh):
    in_specs = (
        P("pp", "ctx", "tp"),
        P("pp", ("ctx", "tp"), None),
        P("pp", None),
        P("pp", None, "tp"),
        P("pp", "tp", None),
        P("pp", ("ctx", "tp"), None),
        P("pp", None),
    )
    out_specs = P("pp", ("ctx", "tp"), None)
    return jax.shard_map(local, mesh=mesh, in_specs=in_specs, out_specs=out_specs, check_vma=False)
```

```python
import functools
import math

import jax
import jax.numpy as jnp
import numpy as np
from jax import lax
from jax.experimental import pallas as pl
from jax.experimental.pallas import tpu as pltpu
from jax.sharding import PartitionSpec as P

NOPE = 128
ROPE = 64
VDIM = 128
LATENT = 512
LANES = 128

score_scale = 0.135
SCALE2 = score_scale * math.log2(math.e)

HEADS_STEP = 8
MIB = 1024 * 1024
PREPARE_VMEM = 16 * MIB
PROJECT_VMEM = 24 * MIB
ATTEND_VMEM = 40 * MIB
ADD_VMEM = 8 * MIB
FINAL_FLOPS = 10**10
FIRST_SHARE = 50
PIECES = 2
TILE = 896


def row_places(order_ref, first, count, block_len):
    return order_ref[first // block_len] * block_len + first % block_len


def rope_tables(places):
    lane = lax.broadcasted_iota(jnp.int32, (places.shape[0], LANES), 1)
    angles = places.astype(jnp.float32) * lane_freqs()
    cos, sin = jnp.cos(angles), jnp.sin(angles)
    half = ROPE // 2
    return (
        jnp.where(lane < ROPE, cos, 0.0),
        jnp.where((lane >= half) & (lane < ROPE), sin, 0.0),
        jnp.where(lane < half, -sin, 0.0),
    )


def turned(x, cos, sin_up, sin_down):
    half = ROPE // 2
    return (
        x * cos + pltpu.roll(x, half, 1) * sin_up + pltpu.roll(x, LANES - half, 1) * sin_down
    ).astype(jnp.bfloat16)


def lane_freqs():
    half = ROPE // 2
    lane = lax.broadcasted_iota(jnp.int32, (1, LANES), 1) % half
    freqs = jnp.zeros((1, LANES), jnp.float32)
    for j in range(half):
        freqs = jnp.where(lane == j, np.float32(10000.0 ** (-2.0 * j / ROPE)), freqs)
    return freqs


def own_keys_kernel(block_len, order_ref, latent_ref, gain_ref, out_ref):
    rows = latent_ref.shape[0]
    first = (lax.axis_index("ctx") * lax.axis_size("tp") + lax.axis_index("tp")) * rows
    places = row_places(order_ref, first, rows, block_len) + lax.broadcasted_iota(jnp.int32, (rows, 1), 0)
    compressed = latent_ref[:, :LATENT].astype(jnp.float32)
    scale_rows = lax.rsqrt(jnp.mean(compressed * compressed, axis=-1, keepdims=True) + 1e-06)
    out_ref[:, :LATENT] = (compressed * scale_rows * gain_ref[...]).astype(jnp.bfloat16)
    rope = jnp.concatenate(
        [latent_ref[:, LATENT:].astype(jnp.float32), jnp.zeros((rows, LANES - ROPE), jnp.float32)], axis=1
    )
    out_ref[:, LATENT:] = turned(rope, *rope_tables(places))


def own_keys(order_row, latents, gain, block_len):
    return pl.pallas_call(
        functools.partial(own_keys_kernel, block_len),
        out_shape=pltpu.VMEM((latents.shape[0], LATENT + LANES), jnp.bfloat16),
        in_specs=[pl.BlockSpec(memory_space=pltpu.SMEM)] + [pl.BlockSpec(memory_space=pltpu.VMEM)] * 2,
        out_specs=pl.BlockSpec(memory_space=pltpu.VMEM),
        compiler_params=pltpu.CompilerParams(vmem_limit_bytes=60 * MIB),
    )(order_row, latents, gain)


def join_kernel(count, *refs):
    at = 0
    for ref in refs[:count]:
        refs[-1][at : at + ref.shape[0], :] = ref[...]
        at += ref.shape[0]


def join_after(arrays, earlier):
    rows = sum(array.shape[0] for array in arrays)
    return pl.pallas_call(
        functools.partial(join_kernel, len(arrays)),
        out_shape=jax.ShapeDtypeStruct((rows, arrays[0].shape[1]), arrays[0].dtype),
        in_specs=[pl.BlockSpec(memory_space=pltpu.VMEM)] * len(arrays)
        + [pl.BlockSpec(memory_space=pl.ANY)] * len(earlier),
        out_specs=pl.BlockSpec(memory_space=pltpu.VMEM),
        compiler_params=pltpu.CompilerParams(vmem_limit_bytes=16 * 1024 * 1024),
    )(*arrays, *earlier)


def gather_masks():
    masks = [(0, 0)]
    for s in range(lax.axis_size("tp").bit_length() - 1):
        masks = masks + [(c, t ^ (1 << s)) for c, t in masks]
    for s in list(range(1, lax.axis_size("ctx").bit_length() - 1)) + [0]:
        masks = masks + [(c ^ (1 << s), t) for c, t in masks]
    return masks


def gather_keys(own, earlier):
    tp_count, ctx_count = lax.axis_size("tp"), lax.axis_size("ctx")

    def traded(value, axis, step):
        return lax.ppermute(value, axis, [(i, i ^ step) for i in range(lax.axis_size(axis))])

    pieces = [own]
    for s in range(tp_count.bit_length() - 1):
        held = own if s == 0 else join_after(pieces, [])
        pieces = [held, traded(held, "tp", 1 << s)]
    pieces[-1] = join_after(pieces[-1:], earlier)
    for s in list(range(1, ctx_count.bit_length() - 1)) + [0]:
        pieces = pieces + [traded(piece, "ctx", 1 << s) for piece in pieces]
    return pieces


def prepare_kernel(block_len, key_rows, masks, order_ref, q_hbm, out_ref, bias_ref, q_ref, semaphore):
    rows = q_ref.shape[0]
    fetch = pltpu.make_async_copy(q_hbm, q_ref, semaphore)
    fetch.start()
    tp_count = lax.axis_size("tp")
    ctx, tp = lax.axis_index("ctx"), lax.axis_index("tp")
    row = lax.broadcasted_iota(jnp.int32, (rows, 1), 0)
    places = jnp.zeros((rows, 1), jnp.int32)
    for b in range(rows // block_len):
        base = row_places(order_ref, ctx * rows + b * block_len, block_len, block_len)
        places = jnp.where(row // block_len == b, base + row % block_len, places)
    lane = lax.broadcasted_iota(jnp.int32, (1, LANES), 1)
    group = LANES // key_rows
    for g in range(len(masks) // group):
        keys = jnp.zeros((1, LANES), jnp.int32)
        for j in range(group):
            c, t = masks[g * group + j]
            base = row_places(order_ref, ((ctx ^ c) * tp_count + (tp ^ t)) * key_rows, key_rows, block_len)
            keys = jnp.where(lane // key_rows == j, base + lane % key_rows, keys)
        bias_ref[:, g * LANES : (g + 1) * LANES] = jnp.where(keys <= places, 0.0, -1e30)
    tables = rope_tables(places)
    lane = lax.broadcasted_iota(jnp.int32, (rows, LANES), 1)
    fetch.wait()
    per_step = HEADS_STEP // 2
    for pair in range(q_ref.shape[1] // (3 * LANES)):
        step, base, to = pair // per_step, pair * 3 * LANES, pair % per_step * 4 * LANES
        middle = q_ref[:, base + LANES : base + 2 * LANES].astype(jnp.float32)
        out_ref[step, :, to : to + LANES] = q_ref[:, base : base + LANES]
        out_ref[step, :, to + LANES : to + 2 * LANES] = turned(middle, *tables)
        middle = pltpu.roll(middle, ROPE, 1)
        final = pltpu.roll(q_ref[:, base + 2 * LANES : base + 3 * LANES].astype(jnp.float32), ROPE, 1)
        nope = jnp.where(lane < ROPE, middle, final).astype(jnp.bfloat16)
        out_ref[step, :, to + 2 * LANES : to + 3 * LANES] = nope
        out_ref[step, :, to + 3 * LANES : to + 4 * LANES] = turned(final, *tables)


def prepare(order_row, queries, key_rows, masks, block_len):
    rows = queries.shape[0]
    heads = queries.shape[1] // (NOPE + ROPE)
    key_count = key_rows * len(masks)
    return pl.pallas_call(
        functools.partial(prepare_kernel, block_len, key_rows, masks),
        out_shape=[
            jax.ShapeDtypeStruct((heads // HEADS_STEP, rows, HEADS_STEP * 2 * LANES), jnp.bfloat16),
            jax.ShapeDtypeStruct((rows, key_count), jnp.float32),
        ],
        in_specs=[
            pl.BlockSpec(memory_space=pltpu.SMEM),
            pl.BlockSpec(memory_space=pltpu.HBM),
        ],
        out_specs=[pl.BlockSpec(memory_space=pltpu.VMEM)] * 2,
        scratch_shapes=[pltpu.VMEM(queries.shape, queries.dtype), pltpu.SemaphoreType.DMA],
        compiler_params=pltpu.CompilerParams(vmem_limit_bytes=PREPARE_VMEM),
        cost_estimate=pl.CostEstimate(flops=20 * queries.size, bytes_accessed=6 * queries.size, transcendentals=0),
    )(order_row, queries)


def slot_of_dest(dest):
    tp, last = lax.axis_index("tp"), lax.axis_size("tp") - 1
    right_first = jnp.where(dest > tp, last - dest, last - tp + dest)
    left_first = jnp.where(dest < tp, dest, tp + last - dest)
    return jnp.where(dest == tp, last, jnp.where(2 * tp <= last, right_first, left_first))


def attention_kernel(piece_count, steps, *refs):
    q_ref, bias_ref, w_ref, out_w_ref = refs[:4]
    piece_refs = refs[4 : 4 + piece_count]
    rest_refs = refs[4 + piece_count :]
    attention_ref, term_refs = rest_refs[0], rest_refs[1:-4]
    keys_ref, held_ref, columns_ref, semaphores = rest_refs[-4:]
    step = pl.program_id(0)
    block = q_ref.shape[1] // len(term_refs)
    tiles, _, tile = columns_ref.shape

    def column_copy(i):
        return pltpu.make_async_copy(
            out_w_ref.at[:, pl.ds(i * tile, tile)], columns_ref.at[i], semaphores.at[i]
        )

    @pl.when(step == 0)
    def _():
        for i in range(tiles):
            column_copy(i).start()
        at = 0
        for ref in piece_refs:
            keys_ref[at : at + ref.shape[0], :] = ref[...]
            at += ref.shape[0]

    @pl.when(step < steps)
    def _():
        attend_heads(step, q_ref, bias_ref, w_ref, keys_ref, held_ref, len(term_refs))

    @pl.when(step == steps)
    def _():
        wide = held_ref.shape[2]
        for i in range(steps):
            attention_ref[:, i * wide : (i + 1) * wide] = held_ref[i]
        for i in range(tiles):
            column_copy(i).wait()

    @pl.when(step >= steps)
    def _():
        made = jnp.dot(attention_ref[...], columns_ref[step - steps], preferred_element_type=jnp.float32)
        for i, out in enumerate(term_refs):
            out[...] = made[i * block : (i + 1) * block].astype(out.dtype)


def attend_heads(step, q_ref, bias_ref, w_ref, keys_ref, held_ref, blocks):
    half = keys_ref.shape[0] // 2
    block = q_ref.shape[1] // blocks
    produced = [
        jnp.dot(
            keys_ref[part * half : (part + 1) * half, :LATENT], w_ref[...], preferred_element_type=jnp.float32
        ).astype(jnp.bfloat16)
        for part in range(2)
    ]
    key_rope = [keys_ref[part * half : (part + 1) * half, LATENT:] for part in range(2)]
    ones = jnp.ones((half, LANES), jnp.bfloat16)

    def scores(h):
        base = h * (NOPE + VDIM)
        return [
            lax.dot_general(
                q_ref[step, :, h * 2 * LANES : (h + 1) * 2 * LANES],
                jnp.concatenate([made[:, base : base + NOPE], rope], axis=1),
                (((1,), (1,)), ((), ())),
                preferred_element_type=jnp.float32,
            )
            for made, rope in zip(produced, key_rope)
        ]

    def weigh(found):
        found = [found[0] + bias_ref[:, :half], found[1] + bias_ref[:, half:]]
        top = jnp.max(jnp.maximum(found[0], found[1]), axis=1, keepdims=True)
        return [jnp.exp2((part - top) * SCALE2).astype(jnp.bfloat16) for part in found]

    def finish(h, weights):
        base = h * (NOPE + VDIM) + NOPE
        summed = sum(
            jnp.dot(
                part,
                jnp.concatenate([made[:, base : base + VDIM], ones], axis=1),
                preferred_element_type=jnp.float32,
            )
            for part, made in zip(weights, produced)
        )
        result = (summed[:, :VDIM] / summed[:, VDIM : VDIM + 1]).astype(held_ref.dtype)
        for dest in range(blocks):
            at = pl.multiple_of(slot_of_dest(dest) * block, block)
            held_ref[step, pl.ds(at, block), h * VDIM : (h + 1) * VDIM] = result[dest * block : (dest + 1) * block]

    found, weights = scores(0), None
    for h in range(HEADS_STEP):
        following = scores(h + 1) if h + 1 < HEADS_STEP else None
        now = weigh(found)
        if h > 0:
            finish(h - 1, weights)
        found, weights = following, now
    finish(HEADS_STEP - 1, weights)


def column_tile(lo, size, most):
    return max(t for t in range(LANES, most + 1, LANES) if size % t == 0 and lo % t == 0)


def attend(queries, bias, pieces, up_weights, out_weights, size, blocks):
    rows, key_count = bias.shape
    steps = queries.shape[0]
    heads = steps * HEADS_STEP
    depth = heads * VDIM
    tile = column_tile(0, size, 4 * TILE)
    head_step = lambda i: jnp.minimum(i, steps - 1)
    column_step = lambda i: jnp.maximum(i - steps, 0)
    whole = lambda shape: pl.BlockSpec(shape, lambda i: (0, 0))
    return pl.pallas_call(
        functools.partial(attention_kernel, len(pieces), steps),
        grid=(steps + size // tile,),
        out_shape=[
            jax.ShapeDtypeStruct((rows, depth), jnp.bfloat16),
        ]
        + [pltpu.VMEM((rows // blocks, size), jnp.bfloat16)] * blocks,
        in_specs=[
            pl.BlockSpec(memory_space=pltpu.VMEM),
            pl.BlockSpec(memory_space=pltpu.VMEM),
            pl.BlockSpec((LATENT, HEADS_STEP * (NOPE + VDIM)), lambda i: (0, head_step(i))),
            pl.BlockSpec(memory_space=pltpu.HBM),
        ]
        + [pl.BlockSpec(memory_space=pltpu.VMEM)] * len(pieces),
        out_specs=[pl.BlockSpec(memory_space=pltpu.VMEM)]
        + [pl.BlockSpec((rows // blocks, tile), lambda i: (0, column_step(i)))] * blocks,
        scratch_shapes=[
            pltpu.VMEM((key_count, LATENT + LANES), jnp.bfloat16),
            pltpu.VMEM((steps, rows, HEADS_STEP * VDIM), jnp.bfloat16),
            pltpu.VMEM((size // tile, depth, tile), jnp.bfloat16),
            pltpu.SemaphoreType.DMA((size // tile,)),
        ],
        compiler_params=pltpu.CompilerParams(vmem_limit_bytes=ATTEND_VMEM),
        cost_estimate=pl.CostEstimate(
            flops=2 * heads * key_count * (LATENT * 256 + rows * 512) + 2 * rows * depth * size,
            bytes_accessed=2 * (queries.size + up_weights.size + depth * size),
            transcendentals=heads * rows * key_count,
        ),
    )(queries, bias, up_weights, out_weights, *pieces)


def project_kernel(x_ref, upper_ref, lower_ref, *out_refs):
    block, half = out_refs[0].shape[0], upper_ref.shape[0]
    made = jnp.dot(x_ref[:, :half], upper_ref[...], preferred_element_type=jnp.float32)
    made = made + jnp.dot(x_ref[:, half:], lower_ref[...], preferred_element_type=jnp.float32)
    for i, out in enumerate(out_refs):
        out[...] = made[i * block : (i + 1) * block].astype(out.dtype)


def project(rows, weights, lo, size, blocks):
    count, depth = rows.shape
    tile = column_tile(lo, size, 2 * TILE)
    block = count // blocks
    return pl.pallas_call(
        project_kernel,
        grid=(size // tile,),
        out_shape=[pltpu.VMEM((block, size), jnp.bfloat16)] * blocks,
        in_specs=[
            pl.BlockSpec((count, depth), lambda i: (0, 0)),
            pl.BlockSpec((depth // 2, tile), lambda i: (0, i + lo // tile)),
            pl.BlockSpec((depth // 2, tile), lambda i: (1, i + lo // tile)),
        ],
        out_specs=[pl.BlockSpec((block, tile), lambda i: (0, i))] * blocks,
        compiler_params=pltpu.CompilerParams(vmem_limit_bytes=PROJECT_VMEM),
        cost_estimate=pl.CostEstimate(
            flops=2 * count * depth * size, bytes_accessed=2 * depth * size, transcendentals=0
        ),
    )(rows, weights, weights)


def total_of(refs, flag_ref, always):
    total = jnp.zeros(refs[0].shape, jnp.float32)
    for i, ref in enumerate(refs):
        value = ref[...].astype(jnp.float32)
        total = total + (value if i < always else jnp.where(flag_ref[i - always] > 0, value, 0.0))
    return total.astype(jnp.bfloat16)


def add_kernel(count, *refs):
    refs[-1][...] = total_of(refs[:count], None, count)


def add_after(values, earlier):
    return pl.pallas_call(
        functools.partial(add_kernel, len(values)),
        out_shape=pltpu.VMEM(values[0].shape, jnp.bfloat16),
        in_specs=[pl.BlockSpec(memory_space=pltpu.VMEM)] * len(values)
        + [pl.BlockSpec(memory_space=pl.ANY)] * len(earlier),
        out_specs=pl.BlockSpec(memory_space=pltpu.VMEM),
        compiler_params=pltpu.CompilerParams(vmem_limit_bytes=ADD_VMEM),
    )(*values, *earlier)


def pair_kernel(own_ref, rest_ref, unit_ref, out_ref):
    rows = own_ref.shape[0]
    out_ref[:rows, :] = total_of([own_ref, rest_ref], None, 2)
    out_ref[rows:, :] = unit_ref[...]


def pair_up(own, rest, unit):
    rows, size = own.shape
    return pl.pallas_call(
        pair_kernel,
        out_shape=pltpu.VMEM((2 * rows, size), jnp.bfloat16),
        in_specs=[pl.BlockSpec(memory_space=pltpu.VMEM)] * 3,
        out_specs=pl.BlockSpec(memory_space=pltpu.VMEM),
        compiler_params=pltpu.CompilerParams(vmem_limit_bytes=ADD_VMEM),
    )(own, rest, unit)


def finish_kernel(lo, count, flag_ref, pair_ref, *refs):
    out_hbm, held_ref, semaphore = refs[-3:]
    rows, size = held_ref.shape
    held_ref[...] = total_of([pair_ref.at[:rows, :], *refs[:count]], flag_ref, 1)
    copy = pltpu.make_async_copy(held_ref, out_hbm.at[:, pl.ds(lo, size)], semaphore)
    copy.start()
    copy.wait()


def finish(flags, pair, flagged, lo, width, before):
    rows, size = flagged[0].shape
    operands = [flags, pair, *flagged] + before
    return pl.pallas_call(
        functools.partial(finish_kernel, lo, len(flagged)),
        out_shape=jax.ShapeDtypeStruct((rows, width), jnp.bfloat16),
        in_specs=[pl.BlockSpec(memory_space=pltpu.SMEM)]
        + [pl.BlockSpec(memory_space=pltpu.VMEM)] * (1 + len(flagged))
        + [pl.BlockSpec(memory_space=pl.ANY)] * len(before),
        out_specs=pl.BlockSpec(memory_space=pl.ANY),
        scratch_shapes=[pltpu.VMEM((rows, size), jnp.bfloat16), pltpu.SemaphoreType.DMA],
        input_output_aliases={len(operands) - 1: 0} if before else {},
        compiler_params=pltpu.CompilerParams(vmem_limit_bytes=ADD_VMEM),
        cost_estimate=pl.CostEstimate(flops=FINAL_FLOPS, bytes_accessed=0, transcendentals=0),
    )(*operands)


def local(queries, latents, latent_gain, w_ukv, w_o, residual, block_order):
    tp = lax.axis_index("tp")
    tp_count = lax.axis_size("tp")
    last = tp_count - 1
    tok_dev, lat_rows, width = queries.shape[1], latents.shape[1], w_o.shape[2]
    order_row = block_order[0]
    block_len = tok_dev * lax.axis_size("ctx") // order_row.shape[0]
    tile = column_tile(0, width, TILE)
    first_size = -(-width * FIRST_SHARE // (100 * tile)) * tile
    spans = [(0, first_size), (first_size, width - first_size)]

    turned_queries, bias = prepare(order_row, queries[0], lat_rows, gather_masks(), block_len)
    pieces = gather_keys(own_keys(order_row, latents[0], latent_gain, block_len), [turned_queries, bias])
    attention, *first_terms = attend(turned_queries, bias, pieces, w_ukv[0], w_o[0], first_size, tp_count)

    def slot_of(hop, unit):
        return unit if 2 * hop < last else hop + unit

    def send(hop, value, across):
        steps = [(hop, hop + 1), (last - hop, last - hop - 1)]
        if not across:
            return lax.ppermute(value, "tp", steps)
        return lax.ppermute(
            value, ("tp", "pp"), [(2 * i + p, 2 * j + 1 - p) for i, j in steps for p in range(2)]
        )

    def flags_of(*conditions):
        return jnp.stack(conditions).astype(jnp.int32)

    terms = [first_terms] + [project(attention, w_o[0], *span, tp_count) for span in spans[1:]]
    got, ahead = {}, {}
    for i in range(PIECES):
        for unit in range(last - 1):
            got[0, unit, i] = send(0, terms[i][slot_of(0, unit)], False)
        lo, size = spans[i]
        rest = residual[0][:, lo : lo + size]
        both = pair_up(terms[i][last], rest, terms[i][slot_of(0, last - 1)])
        ahead[i] = lax.ppermute(both, "pp", [(0, 1), (1, 0)])
        got[0, last - 1, i] = send(0, ahead[i][rest.shape[0] :], False)
    before = []
    for stage in range(1, last):
        for i in range(PIECES):
            for hop in range(stage, 0, -1):
                unit = stage - hop
                if unit >= last - hop:
                    continue
                if (stage, hop, i) == (2, 1, 0):
                    before = before + [ahead[0]]
                summed = add_after([terms[i][slot_of(hop, unit)], got[hop - 1, unit, i]], before)
                before = [summed]
                got[hop, unit, i] = send(hop, summed, unit == last - 1 - hop)

    flags = flags_of(*[(tp == hop + 1) | (tp == last - hop - 1) for hop in range(last)])
    out = []
    for i in range(PIECES):
        ended = [got[hop, last - 1 - hop, i] for hop in range(last)]
        out = [finish(flags, ahead[i], ended, spans[i][0], width, out)]
    return out[0][None]


def solution(mesh):
    in_specs = (
        P("pp", "ctx", "tp"),
        P("pp", ("ctx", "tp"), None),
        P("pp", None),
        P("pp", None, "tp"),
        P("pp", "tp", None),
        P("pp", ("ctx", "tp"), None),
        P("pp", None),
    )
    out_specs = P("pp", ("ctx", "tp"), None)
    return jax.shard_map(local, mesh=mesh, in_specs=in_specs, out_specs=out_specs, check_vma=False)
```

```python
import functools
import math

import jax
import jax.numpy as jnp
import numpy as np
from jax import lax
from jax.experimental import pallas as pl
from jax.experimental.pallas import tpu as pltpu
from jax.sharding import PartitionSpec as P

NOPE = 128
ROPE = 64
VDIM = 128
LATENT = 512
LANES = 128

score_scale = 0.135
SCALE2 = score_scale * math.log2(math.e)

HEADS_STEP = 8
MIB = 1024 * 1024
PREPARE_VMEM = 16 * MIB
PROJECT_VMEM = 24 * MIB
ATTEND_VMEM = 40 * MIB
ADD_VMEM = 8 * MIB
FINAL_FLOPS = 10**10
FIRST_SHARE = 50
PIECES = 2
TILE = 896


def row_places(order_ref, first, count, block_len):
    return order_ref[first // block_len] * block_len + first % block_len


def rope_tables(places):
    lane = lax.broadcasted_iota(jnp.int32, (places.shape[0], LANES), 1)
    angles = places.astype(jnp.float32) * lane_freqs()
    cos, sin = jnp.cos(angles), jnp.sin(angles)
    half = ROPE // 2
    return (
        jnp.where(lane < ROPE, cos, 0.0),
        jnp.where((lane >= half) & (lane < ROPE), sin, 0.0),
        jnp.where(lane < half, -sin, 0.0),
    )


def turned(x, cos, sin_up, sin_down):
    half = ROPE // 2
    return (
        x * cos + pltpu.roll(x, half, 1) * sin_up + pltpu.roll(x, LANES - half, 1) * sin_down
    ).astype(jnp.bfloat16)


def lane_freqs():
    half = ROPE // 2
    lane = lax.broadcasted_iota(jnp.int32, (1, LANES), 1) % half
    freqs = jnp.zeros((1, LANES), jnp.float32)
    for j in range(half):
        freqs = jnp.where(lane == j, np.float32(10000.0 ** (-2.0 * j / ROPE)), freqs)
    return freqs


def own_keys_kernel(block_len, order_ref, latent_ref, gain_ref, out_ref):
    rows = latent_ref.shape[0]
    first = (lax.axis_index("ctx") * lax.axis_size("tp") + lax.axis_index("tp")) * rows
    places = row_places(order_ref, first, rows, block_len) + lax.broadcasted_iota(jnp.int32, (rows, 1), 0)
    compressed = latent_ref[:, :LATENT].astype(jnp.float32)
    scale_rows = lax.rsqrt(jnp.mean(compressed * compressed, axis=-1, keepdims=True) + 1e-06)
    out_ref[:, :LATENT] = (compressed * scale_rows * gain_ref[...]).astype(jnp.bfloat16)
    rope = jnp.concatenate(
        [latent_ref[:, LATENT:].astype(jnp.float32), jnp.zeros((rows, LANES - ROPE), jnp.float32)], axis=1
    )
    out_ref[:, LATENT:] = turned(rope, *rope_tables(places))


def own_keys(order_row, latents, gain, block_len):
    return pl.pallas_call(
        functools.partial(own_keys_kernel, block_len),
        out_shape=pltpu.VMEM((latents.shape[0], LATENT + LANES), jnp.bfloat16),
        in_specs=[pl.BlockSpec(memory_space=pltpu.SMEM)] + [pl.BlockSpec(memory_space=pltpu.VMEM)] * 2,
        out_specs=pl.BlockSpec(memory_space=pltpu.VMEM),
        compiler_params=pltpu.CompilerParams(vmem_limit_bytes=60 * MIB),
    )(order_row, latents, gain)


def join_kernel(count, *refs):
    at = 0
    for ref in refs[:count]:
        refs[-1][at : at + ref.shape[0], :] = ref[...]
        at += ref.shape[0]


def join_after(arrays, earlier):
    rows = sum(array.shape[0] for array in arrays)
    return pl.pallas_call(
        functools.partial(join_kernel, len(arrays)),
        out_shape=jax.ShapeDtypeStruct((rows, arrays[0].shape[1]), arrays[0].dtype),
        in_specs=[pl.BlockSpec(memory_space=pltpu.VMEM)] * len(arrays)
        + [pl.BlockSpec(memory_space=pl.ANY)] * len(earlier),
        out_specs=pl.BlockSpec(memory_space=pltpu.VMEM),
        compiler_params=pltpu.CompilerParams(vmem_limit_bytes=16 * 1024 * 1024),
    )(*arrays, *earlier)


def gather_masks():
    masks = [(0, 0)]
    for s in range(lax.axis_size("tp").bit_length() - 1):
        masks = masks + [(c, t ^ (1 << s)) for c, t in masks]
    for s in list(range(1, lax.axis_size("ctx").bit_length() - 1)) + [0]:
        masks = masks + [(c ^ (1 << s), t) for c, t in masks]
    return masks


def gather_keys(own, earlier):
    tp_count, ctx_count = lax.axis_size("tp"), lax.axis_size("ctx")

    def traded(value, axis, step):
        return lax.ppermute(value, axis, [(i, i ^ step) for i in range(lax.axis_size(axis))])

    pieces = [own]
    for s in range(tp_count.bit_length() - 1):
        held = own if s == 0 else join_after(pieces, [])
        pieces = [held, traded(held, "tp", 1 << s)]
    pieces[-1] = join_after(pieces[-1:], earlier)
    for s in list(range(1, ctx_count.bit_length() - 1)) + [0]:
        pieces = pieces + [traded(piece, "ctx", 1 << s) for piece in pieces]
    return pieces


def prepare_kernel(block_len, key_rows, masks, order_ref, q_hbm, out_ref, bias_ref, q_ref, semaphore):
    rows = q_ref.shape[0]
    fetch = pltpu.make_async_copy(q_hbm, q_ref, semaphore)
    fetch.start()
    tp_count = lax.axis_size("tp")
    ctx, tp = lax.axis_index("ctx"), lax.axis_index("tp")
    row = lax.broadcasted_iota(jnp.int32, (rows, 1), 0)
    places = jnp.zeros((rows, 1), jnp.int32)
    for b in range(rows // block_len):
        base = row_places(order_ref, ctx * rows + b * block_len, block_len, block_len)
        places = jnp.where(row // block_len == b, base + row % block_len, places)
    lane = lax.broadcasted_iota(jnp.int32, (1, LANES), 1)
    group = LANES // key_rows
    for g in range(len(masks) // group):
        keys = jnp.zeros((1, LANES), jnp.int32)
        for j in range(group):
            c, t = masks[g * group + j]
            base = row_places(order_ref, ((ctx ^ c) * tp_count + (tp ^ t)) * key_rows, key_rows, block_len)
            keys = jnp.where(lane // key_rows == j, base + lane % key_rows, keys)
        bias_ref[:, g * LANES : (g + 1) * LANES] = jnp.where(keys <= places, 0.0, -1e30)
    tables = rope_tables(places)
    lane = lax.broadcasted_iota(jnp.int32, (rows, LANES), 1)
    fetch.wait()
    per_step = HEADS_STEP // 2
    for pair in range(q_ref.shape[1] // (3 * LANES)):
        step, base, to = pair // per_step, pair * 3 * LANES, pair % per_step * 4 * LANES
        middle = q_ref[:, base + LANES : base + 2 * LANES].astype(jnp.float32)
        out_ref[step, :, to : to + LANES] = q_ref[:, base : base + LANES]
        out_ref[step, :, to + LANES : to + 2 * LANES] = turned(middle, *tables)
        middle = pltpu.roll(middle, ROPE, 1)
        final = pltpu.roll(q_ref[:, base + 2 * LANES : base + 3 * LANES].astype(jnp.float32), ROPE, 1)
        nope = jnp.where(lane < ROPE, middle, final).astype(jnp.bfloat16)
        out_ref[step, :, to + 2 * LANES : to + 3 * LANES] = nope
        out_ref[step, :, to + 3 * LANES : to + 4 * LANES] = turned(final, *tables)


def prepare(order_row, queries, key_rows, masks, block_len):
    rows = queries.shape[0]
    heads = queries.shape[1] // (NOPE + ROPE)
    key_count = key_rows * len(masks)
    return pl.pallas_call(
        functools.partial(prepare_kernel, block_len, key_rows, masks),
        out_shape=[
            pltpu.VMEM((heads // HEADS_STEP, rows, HEADS_STEP * 2 * LANES), jnp.bfloat16),
            jax.ShapeDtypeStruct((rows, key_count), jnp.float32),
        ],
        in_specs=[
            pl.BlockSpec(memory_space=pltpu.SMEM),
            pl.BlockSpec(memory_space=pltpu.HBM),
        ],
        out_specs=[pl.BlockSpec(memory_space=pltpu.VMEM)] * 2,
        scratch_shapes=[pltpu.VMEM(queries.shape, queries.dtype), pltpu.SemaphoreType.DMA],
        compiler_params=pltpu.CompilerParams(vmem_limit_bytes=PREPARE_VMEM),
        cost_estimate=pl.CostEstimate(flops=20 * queries.size, bytes_accessed=6 * queries.size, transcendentals=0),
    )(order_row, queries)


def slot_of_dest(dest):
    tp, last = lax.axis_index("tp"), lax.axis_size("tp") - 1
    right_first = jnp.where(dest > tp, last - dest, last - tp + dest)
    left_first = jnp.where(dest < tp, dest, tp + last - dest)
    return jnp.where(dest == tp, last, jnp.where(2 * tp <= last, right_first, left_first))


def attention_kernel(piece_count, steps, *refs):
    q_ref, bias_ref, w_ref, out_w_ref = refs[:4]
    piece_refs = refs[4 : 4 + piece_count]
    rest_refs = refs[4 + piece_count :]
    attention_ref, term_refs = rest_refs[0], rest_refs[1:-4]
    keys_ref, held_ref, columns_ref, semaphores = rest_refs[-4:]
    step = pl.program_id(0)
    block = q_ref.shape[1] // len(term_refs)
    tiles, _, tile = columns_ref.shape

    def column_copy(i):
        return pltpu.make_async_copy(
            out_w_ref.at[:, pl.ds(i * tile, tile)], columns_ref.at[i], semaphores.at[i]
        )

    @pl.when(step == 0)
    def _():
        for i in range(tiles):
            column_copy(i).start()
        at = 0
        for ref in piece_refs:
            keys_ref[at : at + ref.shape[0], :] = ref[...]
            at += ref.shape[0]

    @pl.when(step < steps)
    def _():
        attend_heads(step, q_ref, bias_ref, w_ref, keys_ref, held_ref, len(term_refs))

    @pl.when(step == steps)
    def _():
        wide = held_ref.shape[2]
        for i in range(steps):
            attention_ref[:, i * wide : (i + 1) * wide] = held_ref[i]
        for i in range(tiles):
            column_copy(i).wait()

    @pl.when(step >= steps)
    def _():
        made = jnp.dot(attention_ref[...], columns_ref[step - steps], preferred_element_type=jnp.float32)
        for i, out in enumerate(term_refs):
            out[...] = made[i * block : (i + 1) * block].astype(out.dtype)


def attend_heads(step, q_ref, bias_ref, w_ref, keys_ref, held_ref, blocks):
    half = keys_ref.shape[0] // 2
    block = q_ref.shape[1] // blocks
    produced = [
        jnp.dot(
            keys_ref[part * half : (part + 1) * half, :LATENT], w_ref[...], preferred_element_type=jnp.float32
        ).astype(jnp.bfloat16)
        for part in range(2)
    ]
    key_rope = [keys_ref[part * half : (part + 1) * half, LATENT:] for part in range(2)]
    ones = jnp.ones((half, LANES), jnp.bfloat16)

    def scores(h):
        base = h * (NOPE + VDIM)
        return [
            lax.dot_general(
                q_ref[step, :, h * 2 * LANES : (h + 1) * 2 * LANES],
                jnp.concatenate([made[:, base : base + NOPE], rope], axis=1),
                (((1,), (1,)), ((), ())),
                preferred_element_type=jnp.float32,
            )
            for made, rope in zip(produced, key_rope)
        ]

    def weigh(found):
        found = [found[0] + bias_ref[:, :half], found[1] + bias_ref[:, half:]]
        top = jnp.max(jnp.maximum(found[0], found[1]), axis=1, keepdims=True)
        return [jnp.exp2((part - top) * SCALE2).astype(jnp.bfloat16) for part in found]

    def finish(h, weights):
        base = h * (NOPE + VDIM) + NOPE
        summed = sum(
            jnp.dot(
                part,
                jnp.concatenate([made[:, base : base + VDIM], ones], axis=1),
                preferred_element_type=jnp.float32,
            )
            for part, made in zip(weights, produced)
        )
        result = (summed[:, :VDIM] / summed[:, VDIM : VDIM + 1]).astype(held_ref.dtype)
        for dest in range(blocks):
            at = pl.multiple_of(slot_of_dest(dest) * block, block)
            held_ref[step, pl.ds(at, block), h * VDIM : (h + 1) * VDIM] = result[dest * block : (dest + 1) * block]

    found, weights = scores(0), None
    for h in range(HEADS_STEP):
        following = scores(h + 1) if h + 1 < HEADS_STEP else None
        now = weigh(found)
        if h > 0:
            finish(h - 1, weights)
        found, weights = following, now
    finish(HEADS_STEP - 1, weights)


def column_tile(lo, size, most):
    return max(t for t in range(LANES, most + 1, LANES) if size % t == 0 and lo % t == 0)


def attend(queries, bias, pieces, up_weights, out_weights, size, blocks):
    rows, key_count = bias.shape
    steps = queries.shape[0]
    heads = steps * HEADS_STEP
    depth = heads * VDIM
    tile = column_tile(0, size, 4 * TILE)
    head_step = lambda i: jnp.minimum(i, steps - 1)
    column_step = lambda i: jnp.maximum(i - steps, 0)
    whole = lambda shape: pl.BlockSpec(shape, lambda i: (0, 0))
    return pl.pallas_call(
        functools.partial(attention_kernel, len(pieces), steps),
        grid=(steps + size // tile,),
        out_shape=[
            jax.ShapeDtypeStruct((rows, depth), jnp.bfloat16),
        ]
        + [pltpu.VMEM((rows // blocks, size), jnp.bfloat16)] * blocks,
        in_specs=[
            pl.BlockSpec(memory_space=pltpu.VMEM),
            pl.BlockSpec(memory_space=pltpu.VMEM),
            pl.BlockSpec((LATENT, HEADS_STEP * (NOPE + VDIM)), lambda i: (0, head_step(i))),
            pl.BlockSpec(memory_space=pltpu.HBM),
        ]
        + [pl.BlockSpec(memory_space=pltpu.VMEM)] * len(pieces),
        out_specs=[pl.BlockSpec(memory_space=pltpu.VMEM)]
        + [pl.BlockSpec((rows // blocks, tile), lambda i: (0, column_step(i)))] * blocks,
        scratch_shapes=[
            pltpu.VMEM((key_count, LATENT + LANES), jnp.bfloat16),
            pltpu.VMEM((steps, rows, HEADS_STEP * VDIM), jnp.bfloat16),
            pltpu.VMEM((size // tile, depth, tile), jnp.bfloat16),
            pltpu.SemaphoreType.DMA((size // tile,)),
        ],
        compiler_params=pltpu.CompilerParams(vmem_limit_bytes=ATTEND_VMEM),
        cost_estimate=pl.CostEstimate(
            flops=2 * heads * key_count * (LATENT * 256 + rows * 512) + 2 * rows * depth * size,
            bytes_accessed=2 * (queries.size + up_weights.size + depth * size),
            transcendentals=heads * rows * key_count,
        ),
    )(queries, bias, up_weights, out_weights, *pieces)


def project_kernel(x_ref, upper_ref, lower_ref, *out_refs):
    block, half = out_refs[0].shape[0], upper_ref.shape[0]
    made = jnp.dot(x_ref[:, :half], upper_ref[...], preferred_element_type=jnp.float32)
    made = made + jnp.dot(x_ref[:, half:], lower_ref[...], preferred_element_type=jnp.float32)
    for i, out in enumerate(out_refs):
        out[...] = made[i * block : (i + 1) * block].astype(out.dtype)


def project(rows, weights, lo, size, blocks):
    count, depth = rows.shape
    tile = column_tile(lo, size, 2 * TILE)
    block = count // blocks
    return pl.pallas_call(
        project_kernel,
        grid=(size // tile,),
        out_shape=[pltpu.VMEM((block, size), jnp.bfloat16)] * blocks,
        in_specs=[
            pl.BlockSpec((count, depth), lambda i: (0, 0)),
            pl.BlockSpec((depth // 2, tile), lambda i: (0, i + lo // tile)),
            pl.BlockSpec((depth // 2, tile), lambda i: (1, i + lo // tile)),
        ],
        out_specs=[pl.BlockSpec((block, tile), lambda i: (0, i))] * blocks,
        compiler_params=pltpu.CompilerParams(vmem_limit_bytes=PROJECT_VMEM),
        cost_estimate=pl.CostEstimate(
            flops=2 * count * depth * size, bytes_accessed=2 * depth * size, transcendentals=0
        ),
    )(rows, weights, weights)


def total_of(refs, flag_ref, always):
    total = jnp.zeros(refs[0].shape, jnp.float32)
    for i, ref in enumerate(refs):
        value = ref[...].astype(jnp.float32)
        total = total + (value if i < always else jnp.where(flag_ref[i - always] > 0, value, 0.0))
    return total.astype(jnp.bfloat16)


def add_kernel(count, *refs):
    refs[-1][...] = total_of(refs[:count], None, count)


def add_after(values, earlier):
    return pl.pallas_call(
        functools.partial(add_kernel, len(values)),
        out_shape=pltpu.VMEM(values[0].shape, jnp.bfloat16),
        in_specs=[pl.BlockSpec(memory_space=pltpu.VMEM)] * len(values)
        + [pl.BlockSpec(memory_space=pl.ANY)] * len(earlier),
        out_specs=pl.BlockSpec(memory_space=pltpu.VMEM),
        compiler_params=pltpu.CompilerParams(vmem_limit_bytes=ADD_VMEM),
    )(*values, *earlier)


def pair_kernel(own_ref, rest_ref, unit_ref, out_ref):
    rows = own_ref.shape[0]
    out_ref[:rows, :] = total_of([own_ref, rest_ref], None, 2)
    out_ref[rows:, :] = unit_ref[...]


def pair_up(own, rest, unit):
    rows, size = own.shape
    return pl.pallas_call(
        pair_kernel,
        out_shape=pltpu.VMEM((2 * rows, size), jnp.bfloat16),
        in_specs=[pl.BlockSpec(memory_space=pltpu.VMEM)] * 3,
        out_specs=pl.BlockSpec(memory_space=pltpu.VMEM),
        compiler_params=pltpu.CompilerParams(vmem_limit_bytes=ADD_VMEM),
    )(own, rest, unit)


def finish_kernel(lo, count, flag_ref, pair_ref, *refs):
    out_hbm, held_ref, semaphore = refs[-3:]
    rows, size = held_ref.shape
    held_ref[...] = total_of([pair_ref.at[:rows, :], *refs[:count]], flag_ref, 1)
    copy = pltpu.make_async_copy(held_ref, out_hbm.at[:, pl.ds(lo, size)], semaphore)
    copy.start()
    copy.wait()


def finish(flags, pair, flagged, lo, width, before):
    rows, size = flagged[0].shape
    operands = [flags, pair, *flagged] + before
    return pl.pallas_call(
        functools.partial(finish_kernel, lo, len(flagged)),
        out_shape=jax.ShapeDtypeStruct((rows, width), jnp.bfloat16),
        in_specs=[pl.BlockSpec(memory_space=pltpu.SMEM)]
        + [pl.BlockSpec(memory_space=pltpu.VMEM)] * (1 + len(flagged))
        + [pl.BlockSpec(memory_space=pl.ANY)] * len(before),
        out_specs=pl.BlockSpec(memory_space=pl.ANY),
        scratch_shapes=[pltpu.VMEM((rows, size), jnp.bfloat16), pltpu.SemaphoreType.DMA],
        input_output_aliases={len(operands) - 1: 0} if before else {},
        compiler_params=pltpu.CompilerParams(vmem_limit_bytes=ADD_VMEM),
        cost_estimate=pl.CostEstimate(flops=FINAL_FLOPS, bytes_accessed=0, transcendentals=0),
    )(*operands)


def local(queries, latents, latent_gain, w_ukv, w_o, residual, block_order):
    tp = lax.axis_index("tp")
    tp_count = lax.axis_size("tp")
    last = tp_count - 1
    tok_dev, lat_rows, width = queries.shape[1], latents.shape[1], w_o.shape[2]
    order_row = block_order[0]
    block_len = tok_dev * lax.axis_size("ctx") // order_row.shape[0]
    tile = column_tile(0, width, TILE)
    first_size = -(-width * FIRST_SHARE // (100 * tile)) * tile
    spans = [(0, first_size), (first_size, width - first_size)]

    turned_queries, bias = prepare(order_row, queries[0], lat_rows, gather_masks(), block_len)
    pieces = gather_keys(own_keys(order_row, latents[0], latent_gain, block_len), [turned_queries, bias])
    attention, *first_terms = attend(turned_queries, bias, pieces, w_ukv[0], w_o[0], first_size, tp_count)

    def slot_of(hop, unit):
        return unit if 2 * hop < last else hop + unit

    def send(hop, value, across):
        steps = [(hop, hop + 1), (last - hop, last - hop - 1)]
        if not across:
            return lax.ppermute(value, "tp", steps)
        return lax.ppermute(
            value, ("tp", "pp"), [(2 * i + p, 2 * j + 1 - p) for i, j in steps for p in range(2)]
        )

    def flags_of(*conditions):
        return jnp.stack(conditions).astype(jnp.int32)

    terms = [first_terms] + [project(attention, w_o[0], *span, tp_count) for span in spans[1:]]
    got, ahead = {}, {}
    for i in range(PIECES):
        for unit in range(last - 1):
            got[0, unit, i] = send(0, terms[i][slot_of(0, unit)], False)
        lo, size = spans[i]
        rest = residual[0][:, lo : lo + size]
        both = pair_up(terms[i][last], rest, terms[i][slot_of(0, last - 1)])
        ahead[i] = lax.ppermute(both, "pp", [(0, 1), (1, 0)])
        got[0, last - 1, i] = send(0, ahead[i][rest.shape[0] :], False)
    before = []
    for stage in range(1, last):
        for i in range(PIECES):
            for hop in range(stage, 0, -1):
                unit = stage - hop
                if unit >= last - hop:
                    continue
                if (stage, hop, i) == (2, 1, 0):
                    before = before + [ahead[0]]
                summed = add_after([terms[i][slot_of(hop, unit)], got[hop - 1, unit, i]], before)
                before = [summed]
                got[hop, unit, i] = send(hop, summed, unit == last - 1 - hop)

    flags = flags_of(*[(tp == hop + 1) | (tp == last - hop - 1) for hop in range(last)])
    out = []
    for i in range(PIECES):
        ended = [got[hop, last - 1 - hop, i] for hop in range(last)]
        out = [finish(flags, ahead[i], ended, spans[i][0], width, out)]
    return out[0][None]


def solution(mesh):
    in_specs = (
        P("pp", "ctx", "tp"),
        P("pp", ("ctx", "tp"), None),
        P("pp", None),
        P("pp", None, "tp"),
        P("pp", "tp", None),
        P("pp", ("ctx", "tp"), None),
        P("pp", None),
    )
    out_specs = P("pp", ("ctx", "tp"), None)
    return jax.shard_map(local, mesh=mesh, in_specs=in_specs, out_specs=out_specs, check_vma=False)
```
